128 devices in a mesh: dp: 4 (over x), expert: 32 (over z, y, core).
Axes of the slice: x: 4, y: 4, z: 4, core: 2. Of those that a mesh axis runs over, the one named last changes fastest.
Arguments:
- tokens: bfloat16 [16384, 7168], P(('dp', 'expert')), may hold values from -6 to 6
- expert_ids: int32 [16384, 2], P(('dp', 'expert')), may hold values from 0 to 127, all different within a row
- gates: float32 [16384, 2], P(('dp', 'expert')), may hold values from 0.1 to 1
- grad_mixed: bfloat16 [16384, 7168], P(('dp', 'expert')), may hold values from -6 to 6
- w_gate: bfloat16 [32, 7168, 1024], P('expert', None, 'dp'), may hold values from -0.0625 to 0.0625
- w_up: bfloat16 [32, 7168, 1024], P('expert', None, 'dp'), may hold values from -0.0625 to 0.0625
- w_down: bfloat16 [32, 1024, 7168], P('expert', 'dp'), may hold values from -0.09375 to 0.09375
Outputs:
- mixed: bfloat16 [16384, 7168], P(('dp', 'expert'))
- grad_tokens: bfloat16 [16384, 7168], P(('dp', 'expert'))
- grad_gates: float32 [16384, 2], P(('dp', 'expert'))
The draws below stay inside these ranges and needn't reach their ends.
All inputs are finite; a program needn't handle non-finite values.
Results may differ from the reference program's by a relative error of at most 0.02.
Values may be sent and summed in bfloat16 or wider, within the bound.
No kernel may reach another device: no remote copies, remote signals or barrier semaphores. Data moves between devices by JAX's collectives and lax.ppermute only.
A program may use at most 128 MiB of HBM per device.

```python
import math
import jax
import jax.numpy as jnp
from jax import lax

D = 7168
FF = 4096
EXPERTS_ALL = 128
TOP = 2
CAP = 2
QUARTERS = 4
TOK_DEV = 128
EXPERTS = 8
TOKENS = 16384
N_DP = 4
N_EXPERT = 32


def block_scale(own_key, dims, pieces, least, high):
    level, own = 1.0, jax.random.fold_in(own_key, 6)
    for axis_at, shards_of in pieces:
        steps = jnp.exp(jax.random.uniform(jax.random.fold_in(own, axis_at), (shards_of,), jnp.float32, least / len(pieces), high / len(pieces)))
        level = level * jnp.repeat(steps, dims[axis_at] // shards_of).reshape([-1 if axis == axis_at else 1 for axis in range(len(dims))])
    return level


def distinct(key, rows, count, top, lift):
    order = jax.random.permutation(jax.random.fold_in(key, 1), count)
    boost = order
    for power in range(3):
        boost = boost * boost // count
    boost = boost * lift // count
    lots = jax.random.randint(jax.random.fold_in(key, 2), (rows, count), 0, 4096) + boost
    holders = jax.random.permutation(jax.random.fold_in(key, 3), rows)[jnp.arange(count) % rows]
    lots = jnp.where(jnp.arange(rows)[:, None] == holders[None, :], 1 << 14, lots)
    score = lots * count + jnp.arange(count)
    return lax.top_k(score.astype(jnp.int32), top)[1].astype(jnp.int32)


def normal_values(own_key, extent, scale, most, split=(), held_as=jnp.bfloat16):
    factor_of = block_scale(own_key, extent, split, -0.22, 0.18) if split else 1.0
    entries = jax.random.normal(own_key, extent, jnp.float32) * scale * factor_of
    return jnp.minimum(jnp.maximum(entries, -most), most).astype(held_as)


def setup_inputs(seed: int = 0) -> dict:
    splits = jax.random.split(jax.random.key(seed), 8)
    tokens = normal_values(splits[0], (TOKENS, D), 1.0, 6.0, ((0, 128),))
    expert_ids = distinct(splits[1], TOKENS, EXPERTS_ALL, TOP, 128)
    gates = jnp.clip(jnp.exp(math.log(1.0) - 2.3025851 * jax.random.uniform(splits[2], (TOKENS, TOP), jnp.float32) ** block_scale(splits[2], (TOKENS, TOP), ((0, 128),), -0.2, 0.2)), 0.1, 1.0)
    grad_mixed = normal_values(splits[3], (TOKENS, D), 1.0, 6.0, ((0, 128),))
    w_gate = normal_values(splits[4], (N_EXPERT, D, FF // QUARTERS), D ** -0.5, 0.0625, ((0, 32), (2, 4)))
    w_up = normal_values(splits[5], (N_EXPERT, D, FF // QUARTERS), D ** -0.5, 0.0625, ((0, 32), (2, 4)))
    w_down = normal_values(splits[6], (N_EXPERT, FF // QUARTERS, D), FF ** -0.5, 0.09375, ((0, 32), (1, 4)))
    return {"tokens": tokens, "expert_ids": expert_ids, "gates": gates, "grad_mixed": grad_mixed, "w_gate": w_gate, "w_up": w_up, "w_down": w_down}


def shard_sum(lefts, rights):
    fdev = FF // (QUARTERS * N_DP)
    rows = lefts[0].shape[0]
    total = jnp.zeros((rows, D), jnp.float32)
    for quarter in range(QUARTERS):
        def step(acc, part):
            start = (quarter * N_DP + part) * fdev
            term = jnp.zeros((rows, D), jnp.float32)
            for left, right in zip(lefts, rights):
                piece_left = lax.dynamic_slice_in_dim(left, start, fdev, 1)
                piece_right = lax.dynamic_slice_in_dim(right, start, fdev, 0)
                term = term + jnp.dot(piece_left, piece_right, preferred_element_type=jnp.float32)
            rounded = lax.optimization_barrier(term.astype(jnp.bfloat16))
            return acc + rounded.astype(jnp.float32), None
        inner, unused = lax.scan(step, jnp.zeros((rows, D), jnp.float32), jnp.arange(N_DP, dtype=jnp.int32))
        rounded = lax.optimization_barrier(inner.astype(jnp.bfloat16))
        total = total + rounded.astype(jnp.float32)
    return total


def reference(tokens, expert_ids, gates, grad_mixed, w_gate, w_up, w_down):
    blocks = N_DP * N_EXPERT
    ids = expert_ids.reshape(blocks, TOK_DEV, TOP)
    chosen = jnp.concatenate([ids[:, :, 0], ids[:, :, 1]], axis=1)
    gate_blocks = gates.reshape(blocks, TOK_DEV, TOP)
    gate_flat = jnp.concatenate([gate_blocks[:, :, 0], gate_blocks[:, :, 1]], axis=1)
    onehot = (chosen[:, :, None] == jnp.arange(EXPERTS, dtype=jnp.int32)[None, None, :]).astype(jnp.int32)
    before = jnp.cumsum(onehot, axis=1) - onehot
    place = jnp.sum(before * onehot, axis=2)
    kept = (jnp.sum(onehot, axis=2) > 0) & (place < CAP)
    block_index = jnp.arange(blocks, dtype=jnp.int32)[:, None]
    local = jnp.concatenate([jnp.arange(TOK_DEV, dtype=jnp.int32), jnp.arange(TOK_DEV, dtype=jnp.int32)])[None, :]
    choice_of = jnp.concatenate([jnp.zeros((TOK_DEV,), jnp.int32), jnp.ones((TOK_DEV,), jnp.int32)])[None, :]
    token_global = block_index * TOK_DEV + local
    total_slots = blocks * EXPERTS * CAP
    target = jnp.where(kept, block_index * (EXPERTS * CAP) + chosen * CAP + place, total_slots).reshape(-1)
    slot_tok = jnp.full((total_slots,), -1, jnp.int32).at[target].set(token_global.reshape(-1), mode="drop").reshape(blocks, EXPERTS, CAP)
    slot_gate = jnp.zeros((total_slots,), jnp.float32).at[target].set(gate_flat.reshape(-1), mode="drop").reshape(blocks, EXPERTS, CAP)
    slot_k = jnp.zeros((total_slots,), jnp.int32).at[target].set(jnp.broadcast_to(choice_of, (blocks, 2 * TOK_DEV)).reshape(-1), mode="drop").reshape(blocks, EXPERTS, CAP)
    mixed_acc = tokens.astype(jnp.float32)
    grad_acc = grad_mixed.astype(jnp.float32)
    gate_grad = jnp.zeros((TOKENS, TOP), jnp.float32)
    zero_bf = jnp.zeros((), jnp.bfloat16)
    for expert in range(EXPERTS):
        rows_tok = slot_tok[:, expert, :].reshape(-1)
        valid = rows_tok >= 0
        safe = jnp.maximum(rows_tok, 0)
        weight_row = jnp.where(valid, slot_gate[:, expert, :].reshape(-1), 0.0)
        which = slot_k[:, expert, :].reshape(-1)
        rows = jnp.where(valid[:, None], tokens[safe], zero_bf)
        gate_block = w_gate[expert * QUARTERS:(expert + 1) * QUARTERS]
        up_block = w_up[expert * QUARTERS:(expert + 1) * QUARTERS]
        down_full = w_down[expert * QUARTERS:(expert + 1) * QUARTERS].reshape(FF, D)
        gate_full = jnp.transpose(gate_block, (1, 0, 2)).reshape(D, FF)
        up_full = jnp.transpose(up_block, (1, 0, 2)).reshape(D, FF)
        gate_back = jnp.transpose(gate_block, (0, 2, 1)).reshape(FF, D)
        up_back = jnp.transpose(up_block, (0, 2, 1)).reshape(FF, D)
        pre_gate = jnp.dot(rows, gate_full, preferred_element_type=jnp.float32)
        pre_up = jnp.dot(rows, up_full, preferred_element_type=jnp.float32)
        hidden = (jax.nn.silu(pre_gate) * pre_up).astype(jnp.bfloat16)
        expert_out = shard_sum((hidden,), (down_full,))
        mixed_acc = mixed_acc.at[safe].add(weight_row[:, None] * expert_out)
        dy_rows = grad_mixed[safe].astype(jnp.float32)
        inner = jnp.where(valid, jnp.sum(dy_rows * expert_out, axis=1), 0.0)
        gate_grad = gate_grad.at[safe, which].add(inner)
        scaled = (weight_row[:, None] * dy_rows).astype(jnp.bfloat16)
        grad_hidden = jnp.dot(scaled, down_full.T, preferred_element_type=jnp.float32)
        sig = jax.nn.sigmoid(pre_gate)
        grad_a = (grad_hidden * pre_up * sig * (1.0 + pre_gate * (1.0 - sig))).astype(jnp.bfloat16)
        grad_b = (grad_hidden * pre_gate * sig).astype(jnp.bfloat16)
        grad_rows = shard_sum((grad_a, grad_b), (gate_back, up_back))
        grad_acc = grad_acc.at[safe].add(jnp.where(valid[:, None], grad_rows, 0.0))
    return mixed_acc.astype(jnp.bfloat16), grad_acc.astype(jnp.bfloat16), gate_grad
```

```python
import functools

import jax
import jax.numpy as jnp
from jax import lax
from jax.experimental import pallas as pl
from jax.experimental.pallas import tpu as pltpu
from jax.sharding import PartitionSpec as P

BF = jnp.bfloat16
F32 = jnp.float32
VMEM = pl.BlockSpec(memory_space=pltpu.VMEM)
ANY = pl.BlockSpec(memory_space=pl.ANY)
LIMIT = 48 * 1024 * 1024
NZ = 4
STEPS = 7


def dot(a, b, dims):
    return lax.dot_general(a, b, (dims, ((), ())), preferred_element_type=F32)


def place_of(index):
    return index // 8, (index // 4) % 2, (index // 2) % 2, index % 2


def index_of(z, h, l, c):
    return ((z * 2 + h) * 2 + l) * 2 + c


def over_expert(value, move):
    pairs = []
    for at in range(32):
        pairs.append((at, index_of(*move(*place_of(at)))))
    return lax.ppermute(value, "expert", pairs)


def other_core(value):
    return over_expert(value, lambda z, h, l, c: (z, h, l, 1 - c))


def other_l(value):
    return over_expert(value, lambda z, h, l, c: (z, h, 1 - l, c))


def out_to(value, i):
    k, r = i // 2, i % 2
    return over_expert(value, lambda z, h, l, c: ((z + k) % NZ, h ^ r, l ^ r, c))


def back_to(value, i):
    k, r = i // 2, i % 2
    return over_expert(value, lambda z, h, l, c: ((z - k) % NZ, h ^ r, l ^ r, c))


def along_x(value, step):
    return lax.ppermute(value, "dp", [(x, (x + step) % 4) for x in range(4)])


def selection(ids, rows, expert, place):
    tok = ids.shape[1]
    up = (lax.broadcasted_iota(jnp.int32, (tok, tok), 0) < lax.broadcasted_iota(jnp.int32, (tok, tok), 1))
    up = jnp.where(up, 1.0, 0.0).astype(BF)
    first = jnp.where(jnp.broadcast_to(ids[0:1, :], (rows, tok)) == expert, 1.0, 0.0)
    second = jnp.where(jnp.broadcast_to(ids[1:2, :], (rows, tok)) == expert, 1.0, 0.0)
    before_first = dot(first.astype(BF), up, ((1,), (0,)))
    before_second = dot(second.astype(BF), up, ((1,), (0,))) + jnp.sum(first, axis=1, keepdims=True)
    want = place.astype(F32)
    sel_first = jnp.where(before_first == want, first, 0.0)
    sel_second = jnp.where(before_second == want, second, 0.0)
    return sel_first, sel_second


def slot_expert(i, z, h):
    return ((z + (i >> 1)) & 3) * 2 + ((h + (i & 1)) & 1)


def dispatch_kernel(half, ids_ref, gates_ref, tok_hbm, grad_hbm, keep_ref, send_ref, tok_v, grad_v, sems):
    at = lax.axis_index("expert")
    core = at & 1
    h = (at >> 2) & 1
    z = at >> 3
    copies = []
    for n, which in enumerate((1 - core, core)):
        cols = pl.ds(pl.multiple_of(which * half, 128), half)
        one = pltpu.make_async_copy(tok_hbm.at[:, cols], tok_v.at[n], sems.at[n, 0])
        two = pltpu.make_async_copy(grad_hbm.at[:, cols], grad_v.at[n], sems.at[n, 1])
        one.start()
        two.start()
        copies.append((one, two))
    rows, tok = 64, ids_ref.shape[1]
    s = lax.broadcasted_iota(jnp.int32, (rows, tok), 0)
    sel_first, sel_second = selection(ids_ref[...], rows, slot_expert(s >> 3, z, h), s & 1)
    mine = ((s >> 1) & 1) == core
    is_grad = ((s >> 2) & 1) == 1
    member = jnp.where(mine, sel_first + sel_second, 0.0)
    gate = jnp.sum(
        sel_first * jnp.broadcast_to(gates_ref[0:1, :], (rows, tok))
        + sel_second * jnp.broadcast_to(gates_ref[1:2, :], (rows, tok)),
        axis=1,
        keepdims=True,
    )
    of_tok = jnp.where(is_grad, 0.0, member).astype(BF)
    of_grad = jnp.where(is_grad, member, 0.0).astype(BF)
    for n, out in enumerate((send_ref, keep_ref)):
        copies[n][0].wait()
        copies[n][1].wait()
        got = dot(of_tok, tok_v[n], ((1,), (0,))) + dot(of_grad, grad_v[n], ((1,), (0,))) * gate
        out[...] = got.astype(BF)


def merge_kernel(keep_ref, recv_ref, *outs):
    both = keep_ref[...].astype(F32) + recv_ref[...].astype(F32)
    for i, out in enumerate(outs):
        out[...] = both[8 * i : 8 * i + 8, :].astype(BF)


def assemble_kernel(*refs):
    msgs, (tok_ref, grad_ref), wide = refs[:8], refs[8:10], refs[10]
    for i, m in enumerate(msgs):
        wide[pl.ds(8 * i, 8), :] = m[...].astype(F32)
    full = wide[...].astype(BF)
    s = lax.broadcasted_iota(jnp.int32, (32, 64), 0)
    t = lax.broadcasted_iota(jnp.int32, (32, 64), 1)
    base = (s >> 2) * 8 + (s & 3)
    tok_ref[...] = dot(jnp.where(t == base, 1.0, 0.0).astype(BF), full, ((1,), (0,))).astype(BF)
    grad_ref[...] = dot(jnp.where(t == base + 4, 1.0, 0.0).astype(BF), full, ((1,), (0,))).astype(BF)


def up_kernel(core_ref, *refs):
    chunks = refs[:8]
    wg_own, wu_own, wg_got, wu_got, out, rows = refs[8:]
    step = pl.program_id(0)
    for n, chunk in enumerate(chunks):
        rows[pl.ds(32 * n, 32), :] = chunk[...]
    x = rows[...]

    @pl.when(step == 0)
    def _():
        out[...] = jnp.zeros_like(out)

    out[:, 0:256] += dot(x, wg_own[0], ((1,), (0,)))
    out[:, 256:512] += dot(x, wg_got[...], ((1,), (0,)))
    out[:, 512:768] += dot(x, wu_own[0], ((1,), (0,)))
    out[:, 768:1024] += dot(x, wu_got[...], ((1,), (0,)))


def summed(mine, got, base):
    return jnp.concatenate(
        [
            mine[:, base : base + 256] + got[:, base + 256 : base + 512],
            mine[:, base + 256 : base + 512] + got[:, base : base + 256],
        ],
        axis=1,
    )


def down_kernel(core_ref, mine, got, wd_own, wd_got, *refs):
    outs, hidden = refs[:8], refs[8]

    @pl.when(pl.program_id(0) == 0)
    def _():
        a = summed(mine, got, 0)
        b = summed(mine, got, 512)
        hidden[...] = (a * jax.nn.sigmoid(a) * b).astype(BF)

    res = dot(hidden[:, 0:256], wd_own[0], ((1,), (0,))) + dot(hidden[:, 256:512], wd_got[...], ((1,), (0,)))
    res = res.astype(BF)
    for n, out in enumerate(outs):
        out[...] = res[32 * n : 32 * n + 32, :]


def down_back_kernel(core_ref, *refs):
    chunks = refs[:8]
    wd_own, wd_got, out, rows = refs[8:]
    for n, chunk in enumerate(chunks):
        rows[pl.ds(32 * n, 32), :] = chunk[...]
    g = rows[...]

    @pl.when(pl.program_id(0) == 0)
    def _():
        out[...] = jnp.zeros_like(out)

    out[:, 0:256] += dot(g, wd_own[0], ((1,), (1,)))
    out[:, 256:512] += dot(g, wd_got[...], ((1,), (1,)))


def up_back_kernel(core_ref, mine, got, g_mine, g_got, wg_own, wu_own, wg_got, wu_got, *refs):
    outs, (ga_ref, gb_ref) = refs[:8], refs[8:]

    @pl.when(pl.program_id(0) == 0)
    def _():
        a = summed(mine, got, 0)
        b = summed(mine, got, 512)
        gh = summed(g_mine, g_got, 0)
        sg = jax.nn.sigmoid(a)
        ga_ref[...] = (gh * b * sg * (1.0 + a * (1.0 - sg))).astype(BF)
        gb_ref[...] = (gh * a * sg).astype(BF)

    res = dot(ga_ref[:, 0:256], wg_own[0], ((1,), (1,)))
    res += dot(ga_ref[:, 256:512], wg_got[...], ((1,), (1,)))
    res += dot(gb_ref[:, 0:256], wu_own[0], ((1,), (1,)))
    res += dot(gb_ref[:, 256:512], wu_got[...], ((1,), (1,)))
    res = res.astype(BF)
    for n, out in enumerate(outs):
        out[...] = res[32 * n : 32 * n + 32, :]


def add_kernel(*refs):
    total = refs[0][...].astype(F32)
    for ref in refs[1:-1]:
        total += ref[...].astype(F32)
    refs[-1][...] = total.astype(BF)


def split_kernel(*refs):
    terms, outs = refs[:-8], refs[-8:]
    total = terms[0][...].astype(F32)
    for ref in terms[1:]:
        total += ref[...].astype(F32)
    for i, out in enumerate(outs):
        out[...] = total[4 * i : 4 * i + 4, :].astype(BF)


def cores_kernel(*refs):
    msgs, (own_ref, send_ref), wide = refs[:8], refs[8:10], refs[10]
    core = lax.axis_index("expert") & 1
    for i, m in enumerate(msgs):
        wide[pl.ds(8 * i, 4), :] = m[...].astype(F32)
        wide[pl.ds(8 * i + 4, 4), :] = jnp.zeros((4, wide.shape[1]), F32)
    full = wide[...].astype(BF)
    s = lax.broadcasted_iota(jnp.int32, (16, 64), 0)
    t = lax.broadcasted_iota(jnp.int32, (16, 64), 1)
    base = (s >> 1) * 8 + (s & 1)
    own_ref[...] = dot(jnp.where(t == base + 2 * core, 1.0, 0.0).astype(BF), full, ((1,), (0,))).astype(BF)
    send_ref[...] = dot(jnp.where(t == base + 2 - 2 * core, 1.0, 0.0).astype(BF), full, ((1,), (0,))).astype(BF)


def slots_of(ids_ref, at):
    rows, tok = 16, ids_ref.shape[1]
    s = lax.broadcasted_iota(jnp.int32, (rows, tok), 0)
    return selection(ids_ref[...], rows, slot_expert(s >> 1, at >> 3, (at >> 2) & 1), s & 1)


def mixed_kernel(half, ids_ref, gates_ref, tok_ref, grad_ref, own_ref, got_ref, out_ref, gg_ref):
    at = lax.axis_index("expert")
    core = at & 1
    sel_first, sel_second = slots_of(ids_ref, at)
    member = (sel_first + sel_second).astype(BF)
    gate = jnp.sum(
        sel_first * jnp.broadcast_to(gates_ref[0:1, :], sel_first.shape)
        + sel_second * jnp.broadcast_to(gates_ref[1:2, :], sel_first.shape),
        axis=1,
        keepdims=True,
    )
    inner = jnp.zeros((16, 1), F32)
    for n, ref in enumerate((own_ref, got_ref)):
        which = core if n == 0 else 1 - core
        cols = pl.ds(pl.multiple_of(which * half, 128), half)
        rows = ref[...].astype(F32)
        inner += jnp.sum(dot(member, grad_ref[:, cols], ((1,), (0,))) * rows, axis=1, keepdims=True)
        scaled = rows * gate
        high = scaled.astype(BF)
        low = (scaled - high.astype(F32)).astype(BF)
        add = dot(member, high, ((0,), (0,))) + dot(member, low, ((0,), (0,)))
        out_ref[:, cols] = (tok_ref[:, cols].astype(F32) + add).astype(BF)
    gg_ref[0:1, :] = jnp.sum(sel_first * inner, axis=0, keepdims=True)
    gg_ref[1:2, :] = jnp.sum(sel_second * inner, axis=0, keepdims=True)


def grad_tokens_kernel(half, ids_ref, grad_ref, own_ref, got_ref, out_ref):
    at = lax.axis_index("expert")
    core = at & 1
    sel_first, sel_second = slots_of(ids_ref, at)
    member = (sel_first + sel_second).astype(BF)
    for n, ref in enumerate((own_ref, got_ref)):
        which = core if n == 0 else 1 - core
        cols = pl.ds(pl.multiple_of(which * half, 128), half)
        add = dot(member, ref[...], ((0,), (0,)))
        out_ref[:, cols] = (grad_ref[:, cols].astype(F32) + add).astype(BF)


def params():
    return pltpu.CompilerParams(vmem_limit_bytes=LIMIT)


def shape(rows, cols, dtype=BF):
    return jax.ShapeDtypeStruct((rows, cols), dtype)


def whole(kernel, outs, args, scratch=(), specs=None):
    return pl.pallas_call(
        kernel,
        out_shape=outs,
        in_specs=specs or [VMEM] * len(args),
        out_specs=jax.tree.map(lambda _: VMEM, outs),
        scratch_shapes=list(scratch),
        compiler_params=params(),
    )(*args)


def stepped(kernel, core, args, in_specs, outs, out_specs, scratch):
    return pl.pallas_call(
        kernel,
        grid_spec=pltpu.PrefetchScalarGridSpec(
            num_scalar_prefetch=1,
            grid=(STEPS,),
            in_specs=in_specs,
            out_specs=out_specs,
            scratch_shapes=scratch,
        ),
        out_shape=outs,
        compiler_params=params(),
    )(core, *args)


def shards(tokens, expert_ids, gates, grad_mixed, w_gate, w_up, w_down):
    tok, width = tokens.shape
    half = width // 2
    block = half // STEPS
    core = lax.axis_index("expert") % 2
    core1 = core.reshape(1).astype(jnp.int32)
    ids_t = expert_ids.T
    gates_t = gates.T

    keep, send = whole(
        functools.partial(dispatch_kernel, half),
        [shape(64, half)] * 2,
        (ids_t, gates_t, tokens, grad_mixed),
        [pltpu.VMEM((2, tok, half), BF), pltpu.VMEM((2, tok, half), BF), pltpu.SemaphoreType.DMA((2, 2))],
        [VMEM, VMEM, ANY, ANY],
    )
    recv = other_core(send)
    wg_got = other_core(lax.dynamic_slice(w_gate[0], ((1 - core) * half, 0), (half, w_gate.shape[2])))
    wu_got = other_core(lax.dynamic_slice(w_up[0], ((1 - core) * half, 0), (half, w_up.shape[2])))
    wd_got = other_core(lax.dynamic_slice(w_down[0], (0, (1 - core) * half), (w_down.shape[1], half)))
    msgs = whole(merge_kernel, [shape(8, half)] * 8, (keep, recv))
    msgs = [msgs[0]] + [out_to(msgs[i], i) for i in range(1, 8)]
    t00, g00 = whole(assemble_kernel, [shape(32, half)] * 2, msgs, [pltpu.VMEM((64, half), F32)])

    t = {(0, 0): t00}
    t[3, 0] = along_x(t00, 1)
    t[1, 0] = along_x(t00, -1)
    t[0, 1] = other_l(t00)
    t[3, 1] = along_x(t[0, 1], 1)
    t[1, 1] = along_x(t[0, 1], -1)
    t[2, 0] = along_x(t[3, 0], 1)
    t[2, 1] = along_x(t[1, 1], -1)
    order = [(a, b) for a in range(4) for b in range(2)]
    g = {(0, 0): g00}
    g[3, 0] = along_x(g00, 1)
    g[1, 0] = along_x(g00, -1)
    g[0, 1] = other_l(g00)
    g[1, 1] = other_l(g[1, 0])
    g[3, 1] = other_l(g[3, 0])
    g[2, 0] = along_x(g[3, 0], 1)
    g[2, 1] = along_x(g[1, 1], -1)

    fdev = w_gate.shape[2]
    chunk_spec = [pl.BlockSpec((32, block), lambda n, c: (0, n))] * 8
    up_own = pl.BlockSpec((1, block, fdev), lambda n, c: (0, c[0] * STEPS + n, 0))
    up_got = pl.BlockSpec((block, fdev), lambda n, c: (n, 0))
    down_own = pl.BlockSpec((1, fdev, block), lambda n, c: (0, 0, c[0] * STEPS + n))
    down_got = pl.BlockSpec((fdev, block), lambda n, c: (0, n))

    def resident(rows, cols):
        return pl.BlockSpec((rows, cols), lambda n, c: (0, 0))

    part = stepped(
        up_kernel,
        core1,
        [t[o] for o in order] + [w_gate, w_up, wg_got, wu_got],
        chunk_spec + [up_own, up_own, up_got, up_got],
        shape(256, 4 * fdev, F32),
        resident(256, 4 * fdev),
        [pltpu.VMEM((256, block), BF)],
    )
    part_got = other_core(part)
    q = stepped(
        down_kernel,
        core1,
        [part, part_got, w_down, wd_got],
        [resident(256, 4 * fdev)] * 2 + [down_own, down_got],
        [shape(32, half)] * 8,
        chunk_spec,
        [pltpu.VMEM((256, 2 * fdev), BF)],
    )
    q = dict(zip(order, q))

    def add(*terms):
        total = terms[0].astype(F32)
        for term in terms[1:]:
            total = total + term.astype(F32)
        return total.astype(BF)

    f20 = along_x(q[2, 0], 1)
    f21 = along_x(q[2, 1], -1)
    f11 = along_x(q[1, 1], 1)
    f30 = along_x(q[3, 0], -1)
    f10 = along_x(add(q[1, 0], f20), 1)
    f31 = along_x(add(q[3, 1], f21), -1)
    s1 = add(q[0, 1], f11, f31)
    out_l = other_l(s1)
    omsgs = whole(split_kernel, [shape(4, half)] * 8, (q[0, 0], f10, f30, out_l))
    omsgs = [omsgs[0]] + [back_to(omsgs[i], i) for i in range(1, 8)]
    o_own, o_send = whole(cores_kernel, [shape(16, half)] * 2, omsgs, [pltpu.VMEM((64, half), F32)])
    o_got = other_core(o_send)

    g_part = stepped(
        down_back_kernel,
        core1,
        [g[o] for o in order] + [w_down, wd_got],
        chunk_spec + [down_own, down_got],
        shape(256, 2 * fdev, F32),
        resident(256, 2 * fdev),
        [pltpu.VMEM((256, block), BF)],
    )
    g_part_got = other_core(g_part)
    p = stepped(
        up_back_kernel,
        core1,
        [part, part_got, g_part, g_part_got, w_gate, w_up, wg_got, wu_got],
        [resident(256, 4 * fdev)] * 2 + [resident(256, 2 * fdev)] * 2 + [up_own, up_own, up_got, up_got],
        [shape(32, half)] * 8,
        chunk_spec,
        [pltpu.VMEM((256, 2 * fdev), BF)] * 2,
    )
    p = dict(zip(order, p))
    h20 = along_x(p[2, 0], -1)
    h21 = along_x(p[2, 1], 1)
    y01 = other_l(p[0, 1])
    y31 = other_l(p[3, 1])
    y11 = other_l(add(p[1, 1], h21))
    x30 = along_x(add(p[3, 0], h20, y31), -1)
    x10 = along_x(add(p[1, 0], y11), 1)
    gmsgs = whole(split_kernel, [shape(4, half)] * 8, (p[0, 0], y01, x30, x10))
    gmsgs = [gmsgs[0]] + [back_to(gmsgs[i], i) for i in range(1, 8)]
    r_own, r_send = whole(cores_kernel, [shape(16, half)] * 2, gmsgs, [pltpu.VMEM((64, half), F32)])
    r_got = other_core(r_send)

    mixed, grad_gates = whole(
        functools.partial(mixed_kernel, half),
        [shape(tok, width), shape(2, tok, F32)],
        (ids_t, gates_t, tokens, grad_mixed, o_own, o_got),
    )
    grad_tokens = whole(
        functools.partial(grad_tokens_kernel, half),
        shape(tok, width),
        (ids_t, grad_mixed, r_own, r_got),
    )
    return mixed, grad_tokens, grad_gates.T


def solution(mesh):
    return jax.shard_map(
        shards,
        mesh=mesh,
        in_specs=(
            P(("dp", "expert"), None),
            P(("dp", "expert"), None),
            P(("dp", "expert"), None),
            P(("dp", "expert"), None),
            P("expert", None, "dp"),
            P("expert", None, "dp"),
            P("expert", "dp", None),
        ),
        out_specs=(P(("dp", "expert"), None), P(("dp", "expert"), None), P(("dp", "expert"), None)),
        check_vma=False,
    )
```

```python
import functools

import jax
import jax.numpy as jnp
from jax import lax
from jax.experimental import pallas as pl
from jax.experimental.pallas import tpu as pltpu
from jax.sharding import PartitionSpec as P

BF = jnp.bfloat16
F32 = jnp.float32
VMEM = pl.BlockSpec(memory_space=pltpu.VMEM)
HBM = pl.BlockSpec(memory_space=pltpu.HBM)
LIMIT = 16 * 1024 * 1024
NZ = 4


def dot(a, b, dims):
    return lax.dot_general(a, b, (dims, ((), ())), preferred_element_type=F32)


def place_of(index):
    return index // 8, (index // 4) % 2, (index // 2) % 2, index % 2


def index_of(z, h, l, c):
    return ((z * 2 + h) * 2 + l) * 2 + c


def over_expert(value, move):
    pairs = []
    for at in range(32):
        pairs.append((at, index_of(*move(*place_of(at)))))
    return lax.ppermute(value, "expert", pairs)


def other_core(value):
    return over_expert(value, lambda z, h, l, c: (z, h, l, 1 - c))


def other_l(value):
    return over_expert(value, lambda z, h, l, c: (z, h, 1 - l, c))


def other_y(value):
    return over_expert(value, lambda z, h, l, c: (z, 1 - h, 1 - l, c))


def other_y_core(value):
    return over_expert(value, lambda z, h, l, c: (z, 1 - h, 1 - l, 1 - c))


def along_z(value, step):
    return over_expert(value, lambda z, h, l, c: ((z + step) % NZ, h, l, c))


def along_x(value, step):
    pairs = []
    for x in range(4):
        for at in range(32):
            to = (x + step) % 4 if at % 2 == 0 else (x - step) % 4
            pairs.append((x * 32 + at, to * 32 + at))
    return lax.ppermute(value, ("dp", "expert"), pairs)


def selection(ids, rows, expert, place):
    tok = ids.shape[1]
    up = (lax.broadcasted_iota(jnp.int32, (tok, tok), 0) < lax.broadcasted_iota(jnp.int32, (tok, tok), 1))
    up = jnp.where(up, 1.0, 0.0).astype(BF)
    first = jnp.where(jnp.broadcast_to(ids[0:1, :], (rows, tok)) == expert, 1.0, 0.0)
    second = jnp.where(jnp.broadcast_to(ids[1:2, :], (rows, tok)) == expert, 1.0, 0.0)
    before_first = dot(first.astype(BF), up, ((1,), (0,)))
    before_second = dot(second.astype(BF), up, ((1,), (0,))) + jnp.sum(first, axis=1, keepdims=True)
    want = place.astype(F32)
    sel_first = jnp.where(before_first == want, first, 0.0)
    sel_second = jnp.where(before_second == want, second, 0.0)
    return sel_first, sel_second


def slot_expert(k, r, z, h):
    return ((z + k) & 3) * 2 + ((h + r) & 1)


def dispatch_kernel(half, ids_ref, gates_ref, tok_hbm, grad_hbm, near_own, far_own, near_other, far_other, tok_v, grad_v, sems):
    at = lax.axis_index("expert")
    core = at & 1
    h = (at >> 2) & 1
    z = at >> 3
    copies = []
    for n, which in enumerate((1 - core, core)):
        cols = pl.ds(pl.multiple_of(which * half, 128), half)
        one = pltpu.make_async_copy(tok_hbm.at[:, cols], tok_v.at[n], sems.at[n, 0])
        two = pltpu.make_async_copy(grad_hbm.at[:, cols], grad_v.at[n], sems.at[n, 1])
        one.start()
        two.start()
        copies.append((one, two))
    rows, tok = 32, ids_ref.shape[1]
    s = lax.broadcasted_iota(jnp.int32, (rows, tok), 0)
    sel_first, sel_second = selection(ids_ref[...], rows, slot_expert((s >> 1) & 3, s >> 4, z, h), s & 1)
    is_grad = ((s >> 3) & 1) == 1
    member = sel_first + sel_second
    gate = jnp.sum(
        sel_first * jnp.broadcast_to(gates_ref[0:1, :], (rows, tok))
        + sel_second * jnp.broadcast_to(gates_ref[1:2, :], (rows, tok)),
        axis=1,
        keepdims=True,
    )
    of_tok = jnp.where(is_grad, 0.0, member).astype(BF)
    of_grad = jnp.where(is_grad, member, 0.0).astype(BF)
    for n, (near, far) in enumerate(((near_other, far_other), (near_own, far_own))):
        copies[n][0].wait()
        copies[n][1].wait()
        got = dot(of_tok, tok_v[n], ((1,), (0,))) + dot(of_grad, grad_v[n], ((1,), (0,))) * gate
        got = got.astype(BF)
        near[...] = got[0:16, :]
        far[...] = got[16:32, :]


def merge_kernel(near_own, near_got, far_own, far_got, *outs):
    core = lax.axis_index("expert") & 1
    full = jnp.concatenate([near_own[...], near_got[...], far_own[...], far_got[...]], axis=0)
    s = lax.broadcasted_iota(jnp.int32, (64, 64), 0)
    t = lax.broadcasted_iota(jnp.int32, (64, 64), 1)
    k, kind, r, c, j = s >> 4, (s >> 3) & 1, (s >> 2) & 1, (s >> 1) & 1, s & 1
    source = r * 32 + ((c + core) & 1) * 16 + kind * 8 + k * 2 + j
    both = dot(jnp.where(t == source, 1.0, 0.0).astype(BF), full, ((1,), (0,))).astype(BF)
    for n, out in enumerate(outs):
        out[...] = both[16 * n : 16 * n + 16, :]


def assemble_kernel(*refs):
    msgs, out = refs[:4], refs[4]
    wide = [m[...].astype(F32) for m in msgs]
    out[...] = jnp.concatenate([m[0:8] for m in wide] + [m[8:16] for m in wide], axis=0).astype(BF)


def weights_kernel(half, flip, wg_ref, wu_ref, wd_ref, out_ref, sems):
    core = lax.axis_index("expert") & 1
    at = (1 - core if flip else core) * half
    rows = pl.ds(pl.multiple_of(at, 256), half)
    copies = [
        pltpu.make_async_copy(wg_ref.at[0, rows, :], out_ref.at[pl.ds(0, half), :], sems.at[0]),
        pltpu.make_async_copy(wu_ref.at[0, rows, :], out_ref.at[pl.ds(half, half), :], sems.at[1]),
    ]
    for n in range(half // 256):
        cols = pl.ds(pl.multiple_of(at + 256 * n, 256), 256)
        into = out_ref.at[pl.ds(2 * half + 256 * n, 256), :]
        copies.append(pltpu.make_async_copy(wd_ref.at[0, :, cols], into, sems.at[2 + n]))
    for copy in copies:
        copy.start()
    for copy in copies:
        copy.wait()


def first_kernel(half, c0, c1, c2, c3, own, got, out, rows, grads):
    for n, chunk in enumerate((c0, c1, c2, c3)):
        rows[pl.ds(32 * n, 32), :] = chunk[0:32, :]
        grads[pl.ds(32 * n, 32), :] = chunk[32:64, :]
    for m, w in enumerate((own, got)):
        at = 256 * m
        out[:, at : at + 256] = dot(rows[...], w[0:half, :], ((1,), (0,)))
        out[:, 512 + at : 768 + at] = dot(rows[...], w[half : 2 * half, :], ((1,), (0,)))
        last = dot(grads[:, 0:256], w[2 * half : 2 * half + 256, :], ((1,), (1,)))
        for n in range(1, half // 256):
            block = w[2 * half + 256 * n : 2 * half + 256 * n + 256, :]
            last += dot(grads[:, 256 * n : 256 * n + 256], block, ((1,), (1,)))
        out[:, 1024 + at : 1280 + at] = last


EARLY = [(0, 0), (3, 0), (1, 0), (0, 1)]
LATE = [(1, 1), (3, 1), (2, 0), (2, 1)]
SENT = [(2, 1), (2, 0), (3, 1), (1, 0)]
KEPT = [(1, 1), (3, 0), (0, 1), (0, 0)]


def second_kernel(half, chunks, *refs):
    parts, (own, got) = refs[:4], refs[4:6]
    outs, (hid_ref, ga_ref, gb_ref) = refs[6:10], refs[10:]
    for n, (a_at, b_at) in enumerate(chunks):
        late = (a_at, b_at) in LATE
        mine, theirs = parts[1 if late else 0], parts[3 if late else 2]
        group = LATE if late else EARLY
        here = pl.ds(32 * group.index((a_at, b_at)), 32)
        there = pl.ds(32 * group.index(((-a_at) % 4, b_at)), 32)

        def both(base):
            return jnp.concatenate(
                [
                    mine[here, base : base + 256] + theirs[there, base + 256 : base + 512],
                    mine[here, base + 256 : base + 512] + theirs[there, base : base + 256],
                ],
                axis=1,
            )

        a, b, gh = both(0), both(512), both(1024)
        sg = jax.nn.sigmoid(a)
        at = pl.ds(32 * n, 32)
        hid_ref[at, :] = (a * sg * b).astype(BF)
        ga_ref[at, :] = (gh * b * sg * (1.0 + a * (1.0 - sg))).astype(BF)
        gb_ref[at, :] = (gh * a * sg).astype(BF)

    for n in range(half // 256):
        at = 256 * n
        res, gres = None, None
        for m, w in enumerate((own, got)):
            cols = slice(256 * m, 256 * m + 256)
            one = dot(hid_ref[:, cols], w[2 * half + at : 2 * half + at + 256, :], ((1,), (0,)))
            two = dot(ga_ref[:, cols], w[at : at + 256, :], ((1,), (1,)))
            two += dot(gb_ref[:, cols], w[half + at : half + at + 256, :], ((1,), (1,)))
            res = one if res is None else res + one
            gres = two if gres is None else gres + two
        res, gres = res.astype(BF), gres.astype(BF)
        for k, out in enumerate(outs):
            out[0:32, at : at + 256] = res[32 * k : 32 * k + 32, :]
            out[32:64, at : at + 256] = gres[32 * k : 32 * k + 32, :]


def finish_kernel(*refs):
    terms, outs = refs[:4], refs[4:]
    total = terms[0][...].astype(F32)
    for ref in terms[1:]:
        total += ref[...].astype(F32)
    for k, out in enumerate(outs):
        out[...] = jnp.concatenate([total[8 * k : 8 * k + 8], total[32 + 8 * k : 40 + 8 * k]], axis=0).astype(BF)


def cores_kernel(*refs):
    msgs, outs = refs[:4], refs[4:]
    core = lax.axis_index("expert") & 1
    full = jnp.concatenate([m[...] for m in msgs], axis=0)
    s = lax.broadcasted_iota(jnp.int32, (64, 64), 0)
    t = lax.broadcasted_iota(jnp.int32, (64, 64), 1)
    r, c, kind, k, j = s >> 5, (s >> 4) & 1, (s >> 3) & 1, (s >> 1) & 3, s & 1
    source = k * 16 + kind * 8 + r * 4 + ((c + core) & 1) * 2 + j
    both = dot(jnp.where(t == source, 1.0, 0.0).astype(BF), full, ((1,), (0,))).astype(BF)
    for n, out in enumerate(outs):
        out[...] = both[16 * n : 16 * n + 16, :]


def tail_kernel(half, ids_ref, gates_ref, tok_ref, grad_ref, near_own, near_got, far_own, far_got, mixed_ref, gt_ref, gg_ref):
    at = lax.axis_index("expert")
    core = at & 1
    rows, tok = 16, ids_ref.shape[1]
    s = lax.broadcasted_iota(jnp.int32, (rows, tok), 0)
    expert = slot_expert((s >> 1) & 3, s >> 3, at >> 3, (at >> 2) & 1)
    sel_first, sel_second = selection(ids_ref[...], rows, expert, s & 1)
    member = (sel_first + sel_second).astype(BF)
    gate = jnp.sum(
        sel_first * jnp.broadcast_to(gates_ref[0:1, :], (rows, tok))
        + sel_second * jnp.broadcast_to(gates_ref[1:2, :], (rows, tok)),
        axis=1,
        keepdims=True,
    )
    inner = jnp.zeros((16, 1), F32)
    for which, near, far in ((core, near_own, far_own), (1 - core, near_got, far_got)):
        cols = pl.ds(pl.multiple_of(which * half, 128), half)
        one, two = near[...].astype(F32), far[...].astype(F32)
        out_rows = jnp.concatenate([one[0:8], two[0:8]], axis=0)
        grad_rows = jnp.concatenate([one[8:16], two[8:16]], axis=0).astype(BF)
        grad = grad_ref[:, cols]
        inner += jnp.sum(dot(member, grad, ((1,), (0,))) * out_rows, axis=1, keepdims=True)
        scaled = out_rows * gate
        high = scaled.astype(BF)
        low = (scaled - high.astype(F32)).astype(BF)
        add = dot(member, high, ((0,), (0,))) + dot(member, low, ((0,), (0,)))
        mixed_ref[:, cols] = (tok_ref[:, cols].astype(F32) + add).astype(BF)
        gt_ref[:, cols] = (grad.astype(F32) + dot(member, grad_rows, ((0,), (0,)))).astype(BF)
    gg_ref[0:1, :] = jnp.sum(sel_first * inner, axis=0, keepdims=True)
    gg_ref[1:2, :] = jnp.sum(sel_second * inner, axis=0, keepdims=True)


def params():
    return pltpu.CompilerParams(vmem_limit_bytes=LIMIT)


def shape(rows, cols, dtype=BF):
    return jax.ShapeDtypeStruct((rows, cols), dtype)


def whole(kernel, outs, args, scratch=(), specs=None):
    return pl.pallas_call(
        kernel,
        out_shape=outs,
        in_specs=specs or [VMEM] * len(args),
        out_specs=jax.tree.map(lambda _: VMEM, outs),
        scratch_shapes=list(scratch),
        compiler_params=params(),
    )(*args)


def weights(half, flip, w_gate, w_up, w_down):
    return whole(
        functools.partial(weights_kernel, half, flip),
        shape(3 * half, w_gate.shape[2]),
        (w_gate, w_up, w_down),
        [pltpu.SemaphoreType.DMA((2 + half // 256,))],
        [HBM] * 3,
    )


def shards(tokens, expert_ids, gates, grad_mixed, w_gate, w_up, w_down):
    tok, width = tokens.shape
    half = width // 2
    ids_t = expert_ids.T
    gates_t = gates.T

    near_own, far_own, near_other, far_other = whole(
        functools.partial(dispatch_kernel, half),
        [shape(16, half)] * 4,
        (ids_t, gates_t, tokens, grad_mixed),
        [pltpu.VMEM((2, tok, half), BF), pltpu.VMEM((2, tok, half), BF), pltpu.SemaphoreType.DMA((2, 2))],
        [VMEM, VMEM, HBM, HBM],
    )
    near_got = other_core(near_other)
    far_got = [other_y(far_own), other_y_core(far_other)]
    near_got, wg_src, wu_src, wd_src = lax.optimization_barrier((near_got, w_gate, w_up, w_down))
    w_got = other_core(weights(half, True, wg_src, wu_src, wd_src))
    msgs = whole(merge_kernel, [shape(16, half)] * 4, (near_own, near_got, *far_got))
    across = along_z(msgs[2], 2)
    msgs = [msgs[0], along_z(msgs[1], 1), across, along_z(msgs[3], 3)]
    t = {(0, 0): whole(assemble_kernel, shape(64, half), msgs)}

    t[0, 1] = other_l(t[0, 0])
    t[3, 0] = along_x(t[0, 0], 1)
    t[1, 0] = along_x(t[0, 0], -1)
    w_got, wg_src, wu_src, wd_src = lax.optimization_barrier((w_got, wg_src, wu_src, wd_src))
    w_own = weights(half, False, wg_src, wu_src, wd_src)
    t[0, 1], t[3, 0], t[1, 0] = lax.optimization_barrier((t[0, 1], t[3, 0], t[1, 0]))
    t[1, 1] = along_x(t[0, 1], -1)
    t[3, 1] = other_l(t[3, 0])
    t[2, 0] = along_x(t[3, 0], 1)
    t[2, 1] = along_x(t[1, 1], -1)

    fdev = w_gate.shape[2]
    parts = []
    for group in (EARLY, LATE):
        parts.append(
            whole(
                functools.partial(first_kernel, half),
                shape(128, 6 * fdev, F32),
                [t[o] for o in group] + [w_own, w_got],
                [pltpu.VMEM((128, half), BF)] * 2,
            )
        )
    parts += [other_core(part) for part in parts]
    q = {}
    for group in (SENT, KEPT):
        res = whole(
            functools.partial(second_kernel, half, group),
            [shape(64, half)] * 4,
            parts + [w_own, w_got],
            [pltpu.VMEM((128, 2 * fdev), BF)] * 3,
        )
        q.update(zip(group, res))

    def add(*terms):
        total = terms[0].astype(F32)
        for term in terms[1:]:
            total = total + term.astype(F32)
        return total.astype(BF)

    f21 = along_x(q[2, 1], 1)
    f20 = along_x(q[2, 0], -1)
    f31 = other_l(q[3, 1])
    q[1, 0], f21 = lax.optimization_barrier((q[1, 0], f21))
    f10 = along_x(q[1, 0], 1)
    f11 = along_x(add(q[1, 1], f21), 1)
    f30 = along_x(add(q[3, 0], f20, f31), -1)
    f01 = other_l(add(q[0, 1], f11))
    back = whole(finish_kernel, [shape(16, half)] * 4, (q[0, 0], f10, f30, f01))
    across = along_z(back[2], -2)
    back = [back[0], along_z(back[1], -1), across, along_z(back[3], -3)]
    near_mine, near_theirs, far_mine, far_theirs = whole(cores_kernel, [shape(16, half)] * 4, back)
    mixed, grad_tokens, grad_gates = whole(
        functools.partial(tail_kernel, half),
        [shape(tok, width), shape(tok, width), shape(2, tok, F32)],
        (ids_t, gates_t, tokens, grad_mixed, near_mine, other_core(near_theirs), other_y(far_mine), other_y_core(far_theirs)),
    )
    return mixed, grad_tokens, grad_gates.T


def solution(mesh):
    return jax.shard_map(
        shards,
        mesh=mesh,
        in_specs=(
            P(("dp", "expert"), None),
            P(("dp", "expert"), None),
            P(("dp", "expert"), None),
            P(("dp", "expert"), None),
            P("expert", None, "dp"),
            P("expert", None, "dp"),
            P("expert", "dp", None),
        ),
        out_specs=(P(("dp", "expert"), None), P(("dp", "expert"), None), P(("dp", "expert"), None)),
        check_vma=False,
    )
```

```python
import functools

import jax
import jax.numpy as jnp
from jax import lax
from jax.experimental import pallas as pl
from jax.experimental.pallas import tpu as pltpu
from jax.sharding import PartitionSpec as P

BF = jnp.bfloat16
F32 = jnp.float32
VMEM = pl.BlockSpec(memory_space=pltpu.VMEM)
HBM = pl.BlockSpec(memory_space=pltpu.HBM)
LIMIT = 16 * 1024 * 1024
BIG = 54 * 1024 * 1024
NZ = 4
HALVES = 2


def dot(a, b, dims):
    return lax.dot_general(a, b, (dims, ((), ())), preferred_element_type=F32)


def place_of(index):
    return index // 8, (index // 4) % 2, (index // 2) % 2, index % 2


def index_of(z, h, l, c):
    return ((z * 2 + h) * 2 + l) * 2 + c


def over_expert(value, move):
    pairs = []
    for at in range(32):
        pairs.append((at, index_of(*move(*place_of(at)))))
    return lax.ppermute(value, "expert", pairs)


def other_core(value):
    return over_expert(value, lambda z, h, l, c: (z, h, l, 1 - c))


def other_l(value):
    return over_expert(value, lambda z, h, l, c: (z, h, 1 - l, c))


def other_y(value):
    return over_expert(value, lambda z, h, l, c: (z, 1 - h, 1 - l, c))


def other_y_core(value):
    return over_expert(value, lambda z, h, l, c: (z, 1 - h, 1 - l, 1 - c))


def along_z(value, step):
    return over_expert(value, lambda z, h, l, c: ((z + step) % NZ, h, l, c))


def along_x(value, step):
    pairs = []
    for x in range(4):
        for at in range(32):
            to = (x + step) % 4 if at % 2 == 0 else (x - step) % 4
            pairs.append((x * 32 + at, to * 32 + at))
    return lax.ppermute(value, ("dp", "expert"), pairs)


def selection(ids, rows, expert, place):
    tok = ids.shape[1]
    up = (lax.broadcasted_iota(jnp.int32, (tok, tok), 0) < lax.broadcasted_iota(jnp.int32, (tok, tok), 1))
    up = jnp.where(up, 1.0, 0.0).astype(BF)
    first = jnp.where(jnp.broadcast_to(ids[0:1, :], (rows, tok)) == expert, 1.0, 0.0)
    second = jnp.where(jnp.broadcast_to(ids[1:2, :], (rows, tok)) == expert, 1.0, 0.0)
    before_first = dot(first.astype(BF), up, ((1,), (0,)))
    before_second = dot(second.astype(BF), up, ((1,), (0,))) + jnp.sum(first, axis=1, keepdims=True)
    want = place.astype(F32)
    sel_first = jnp.where(before_first == want, first, 0.0)
    sel_second = jnp.where(before_second == want, second, 0.0)
    return sel_first, sel_second


def slot_expert(k, r, z, h):
    return ((z + k) & 3) * 2 + ((h + r) & 1)


def weight_copies(half, core, wg_ref, wu_ref, wd_ref, out_ref, sems):
    at = core * half
    rows = pl.ds(pl.multiple_of(at, 256), half)
    copies = [
        pltpu.make_async_copy(wg_ref.at[0, rows, :], out_ref.at[pl.ds(0, half), :], sems.at[0]),
        pltpu.make_async_copy(wu_ref.at[0, rows, :], out_ref.at[pl.ds(half, half), :], sems.at[1]),
    ]
    for n in range(half // 256):
        cols = pl.ds(pl.multiple_of(at + 256 * n, 256), 256)
        into = out_ref.at[pl.ds(2 * half + 256 * n, 256), :]
        copies.append(pltpu.make_async_copy(wd_ref.at[0, :, cols], into, sems.at[2 + n]))
    for copy in copies:
        copy.start()
    return copies


def weights_kernel(half, after_ref, wg_ref, wu_ref, wd_ref, out_ref, sems):
    core = lax.axis_index("expert") & 1
    for copy in weight_copies(half, core, wg_ref, wu_ref, wd_ref, out_ref, sems):
        copy.wait()


def dispatch_kernel(
    half,
    ids_hbm,
    gates_hbm,
    tok_hbm,
    grad_hbm,
    wg_hbm,
    wu_hbm,
    wd_hbm,
    near_own,
    far_own,
    near_other,
    far_other,
    w_send,
    ids_ref,
    gates_ref,
    tok_v,
    grad_v,
    sems,
    small,
    w_sems,
):
    few = [
        pltpu.make_async_copy(ids_hbm, ids_ref, small.at[0]),
        pltpu.make_async_copy(gates_hbm, gates_ref, small.at[1]),
    ]
    for copy in few:
        copy.start()
    at = lax.axis_index("expert")
    core = at & 1
    h = (at >> 2) & 1
    z = at >> 3
    copies = []
    for n, which in enumerate((1 - core, core)):
        cols = pl.ds(pl.multiple_of(which * half, 128), half)
        one = pltpu.make_async_copy(tok_hbm.at[:, cols], tok_v.at[n], sems.at[n, 0])
        two = pltpu.make_async_copy(grad_hbm.at[:, cols], grad_v.at[n], sems.at[n, 1])
        one.start()
        two.start()
        copies.append((one, two))
    big = weight_copies(half, 1 - core, wg_hbm, wu_hbm, wd_hbm, w_send, w_sems)
    for copy in few:
        copy.wait()
    rows, tok = 32, ids_ref.shape[1]
    s = lax.broadcasted_iota(jnp.int32, (rows, tok), 0)
    sel_first, sel_second = selection(ids_ref[...], rows, slot_expert((s >> 1) & 3, s >> 4, z, h), s & 1)
    is_grad = ((s >> 3) & 1) == 1
    member = sel_first + sel_second
    gate = jnp.sum(
        sel_first * jnp.broadcast_to(gates_ref[0:1, :], (rows, tok))
        + sel_second * jnp.broadcast_to(gates_ref[1:2, :], (rows, tok)),
        axis=1,
        keepdims=True,
    )
    of_tok = jnp.where(is_grad, 0.0, member).astype(BF)
    of_grad = jnp.where(is_grad, member, 0.0).astype(BF)
    for n, (near, far) in enumerate(((near_other, far_other), (near_own, far_own))):
        copies[n][0].wait()
        copies[n][1].wait()
        got = dot(of_tok, tok_v[n], ((1,), (0,))) + dot(of_grad, grad_v[n], ((1,), (0,))) * gate
        got = got.astype(BF)
        near[...] = got[0:16, :]
        far[...] = got[16:32, :]
    for copy in big:
        copy.wait()


def merge_kernel(near_own, near_got, far_own, far_got, *outs):
    core = lax.axis_index("expert") & 1
    full = jnp.concatenate([near_own[...], near_got[...], far_own[...], far_got[...]], axis=0)
    s = lax.broadcasted_iota(jnp.int32, (64, 64), 0)
    t = lax.broadcasted_iota(jnp.int32, (64, 64), 1)
    k, kind, r, c, j = s >> 4, (s >> 3) & 1, (s >> 2) & 1, (s >> 1) & 1, s & 1
    source = r * 32 + ((c + core) & 1) * 16 + kind * 8 + k * 2 + j
    both = dot(jnp.where(t == source, 1.0, 0.0).astype(BF), full, ((1,), (0,))).astype(BF)
    for n, out in enumerate(outs):
        out[...] = both[16 * n : 16 * n + 16, :]


def assemble_kernel(m0, m1, m2, m3, *outs):
    wide = [m[...].astype(F32) for m in (m0, m1, m2, m3)]
    full = jnp.concatenate([m[0:8] for m in wide] + [m[8:16] for m in wide], axis=0).astype(BF)
    part = full.shape[1] // len(outs)
    for n, out in enumerate(outs):
        out[...] = full[:, part * n : part * n + part]


def first_kernel(half, *refs):
    chunks, (own, got, out, rows, grads) = refs[:-5], refs[-5:]
    part = chunks[0].shape[1]
    for n, chunk in enumerate(chunks):
        at, cols = pl.ds(32 * (n // HALVES), 32), pl.ds(part * (n % HALVES), part)
        rows[at, cols] = chunk[0:32, :]
        grads[at, cols] = chunk[32:64, :]
    for m, w in enumerate((own, got)):
        at = 256 * m
        out[:, at : at + 256] = dot(rows[...], w[0:half, :], ((1,), (0,)))
        out[:, 512 + at : 768 + at] = dot(rows[...], w[half : 2 * half, :], ((1,), (0,)))
        last = dot(grads[:, 0:256], w[2 * half : 2 * half + 256, :], ((1,), (1,)))
        for n in range(1, half // 256):
            block = w[2 * half + 256 * n : 2 * half + 256 * n + 256, :]
            last += dot(grads[:, 256 * n : 256 * n + 256], block, ((1,), (1,)))
        out[:, 1024 + at : 1280 + at] = last


EARLY = [(0, 0), (3, 0), (1, 0), (0, 1)]
LATE = [(1, 1), (3, 1), (2, 0), (2, 1)]
SENT = [(2, 1), (2, 0), (3, 1), (1, 0)]
KEPT = [(1, 1), (3, 0), (0, 1), (0, 0)]


def second_kernel(half, chunks, *refs):
    parts, (own, got) = refs[:4], refs[4:6]
    outs, (hid_ref, ga_ref, gb_ref) = refs[6:-3], refs[-3:]
    for n, (a_at, b_at) in enumerate(chunks):
        late = (a_at, b_at) in LATE
        mine, theirs = parts[1 if late else 0], parts[3 if late else 2]
        group = LATE if late else EARLY
        here = pl.ds(32 * group.index((a_at, b_at)), 32)
        there = pl.ds(32 * group.index(((-a_at) % 4, b_at)), 32)

        def both(base):
            return jnp.concatenate(
                [
                    mine[here, base : base + 256] + theirs[there, base + 256 : base + 512],
                    mine[here, base + 256 : base + 512] + theirs[there, base : base + 256],
                ],
                axis=1,
            )

        a, b, gh = both(0), both(512), both(1024)
        sg = jax.nn.sigmoid(a)
        at = pl.ds(32 * n, 32)
        hid_ref[at, :] = (a * sg * b).astype(BF)
        ga_ref[at, :] = (gh * b * sg * (1.0 + a * (1.0 - sg))).astype(BF)
        gb_ref[at, :] = (gh * a * sg).astype(BF)

    for n in range(half // 256):
        at = 256 * n
        res, gres = None, None
        for m, w in enumerate((own, got)):
            cols = slice(256 * m, 256 * m + 256)
            one = dot(hid_ref[:, cols], w[2 * half + at : 2 * half + at + 256, :], ((1,), (0,)))
            two = dot(ga_ref[:, cols], w[at : at + 256, :], ((1,), (1,)))
            two += dot(gb_ref[:, cols], w[half + at : half + at + 256, :], ((1,), (1,)))
            res = one if res is None else res + one
            gres = two if gres is None else gres + two
        res, gres = res.astype(BF), gres.astype(BF)
        part = half // HALVES
        for k in range(len(chunks)):
            out = outs[HALVES * k + at // part]
            into = at % part
            out[0:32, into : into + 256] = res[32 * k : 32 * k + 32, :]
            out[32:64, into : into + 256] = gres[32 * k : 32 * k + 32, :]


def finish_kernel(*refs):
    terms, outs = refs[:-4], refs[-4:]
    totals = []
    for n in range(HALVES):
        total = terms[4 * n][...].astype(F32)
        for ref in terms[4 * n + 1 : 4 * n + 4]:
            total += ref[...].astype(F32)
        totals.append(total)
    total = jnp.concatenate(totals, axis=1)
    for k, out in enumerate(outs):
        out[...] = jnp.concatenate([total[8 * k : 8 * k + 8], total[32 + 8 * k : 40 + 8 * k]], axis=0).astype(BF)


def cores_kernel(*refs):
    msgs, outs = refs[:4], refs[4:]
    core = lax.axis_index("expert") & 1
    full = jnp.concatenate([m[...] for m in msgs], axis=0)
    s = lax.broadcasted_iota(jnp.int32, (64, 64), 0)
    t = lax.broadcasted_iota(jnp.int32, (64, 64), 1)
    r, c, kind, k, j = s >> 5, (s >> 4) & 1, (s >> 3) & 1, (s >> 1) & 3, s & 1
    source = k * 16 + kind * 8 + r * 4 + ((c + core) & 1) * 2 + j
    both = dot(jnp.where(t == source, 1.0, 0.0).astype(BF), full, ((1,), (0,))).astype(BF)
    for n, out in enumerate(outs):
        out[...] = both[16 * n : 16 * n + 16, :]


def tail_kernel(half, other, ids_ref, gates_ref, tok_ref, grad_ref, near, far, *refs):
    if other:
        inner_ref, _, _, mixed_hbm, gt_hbm, gg_ref, mixed_ref, gt_ref, sems = refs
    else:
        mixed_hbm, gt_hbm, inner_ref, mixed_ref, gt_ref, sems = refs
    at = lax.axis_index("expert")
    core = at & 1
    which = 1 - core if other else core
    rows, tok = 16, ids_ref.shape[1]
    s = lax.broadcasted_iota(jnp.int32, (rows, tok), 0)
    expert = slot_expert((s >> 1) & 3, s >> 3, at >> 3, (at >> 2) & 1)
    sel_first, sel_second = selection(ids_ref[...], rows, expert, s & 1)
    member = (sel_first + sel_second).astype(BF)
    gate = jnp.sum(
        sel_first * jnp.broadcast_to(gates_ref[0:1, :], (rows, tok))
        + sel_second * jnp.broadcast_to(gates_ref[1:2, :], (rows, tok)),
        axis=1,
        keepdims=True,
    )
    cols = pl.ds(pl.multiple_of(which * half, 128), half)
    one, two = near[...].astype(F32), far[...].astype(F32)
    out_rows = jnp.concatenate([one[0:8], two[0:8]], axis=0)
    grad_rows = jnp.concatenate([one[8:16], two[8:16]], axis=0).astype(BF)
    grad = grad_ref[:, cols]
    gt_ref[...] = (grad.astype(F32) + dot(member, grad_rows, ((0,), (0,)))).astype(BF)
    first = pltpu.make_async_copy(gt_ref, gt_hbm.at[:, cols], sems.at[0])
    first.start()
    scaled = out_rows * gate
    high = scaled.astype(BF)
    low = (scaled - high.astype(F32)).astype(BF)
    add = dot(member, high, ((0,), (0,))) + dot(member, low, ((0,), (0,)))
    mixed_ref[...] = (tok_ref[:, cols].astype(F32) + add).astype(BF)
    second = pltpu.make_async_copy(mixed_ref, mixed_hbm.at[:, cols], sems.at[1])
    second.start()
    inner = jnp.sum(dot(member, grad, ((1,), (0,))) * out_rows, axis=1, keepdims=True)
    if other:
        inner += inner_ref[:, 0:1]
        gg_ref[0:1, :] = jnp.sum(sel_first * inner, axis=0, keepdims=True)
        gg_ref[1:2, :] = jnp.sum(sel_second * inner, axis=0, keepdims=True)
    else:
        inner_ref[...] = jnp.broadcast_to(inner, inner_ref.shape)
    first.wait()
    second.wait()


def shape(rows, cols, dtype=BF):
    return jax.ShapeDtypeStruct((rows, cols), dtype)


def whole(kernel, outs, args, scratch=(), specs=None, limit=LIMIT):
    return pl.pallas_call(
        kernel,
        out_shape=outs,
        in_specs=specs or [VMEM] * len(args),
        out_specs=jax.tree.map(lambda _: VMEM, outs),
        scratch_shapes=list(scratch),
        compiler_params=pltpu.CompilerParams(vmem_limit_bytes=limit),
    )(*args)


def weights(half, after, w_gate, w_up, w_down):
    return whole(
        functools.partial(weights_kernel, half),
        shape(3 * half, w_gate.shape[2]),
        (after, w_gate, w_up, w_down),
        [pltpu.SemaphoreType.DMA((2 + half // 256,))],
        [HBM] * 4,
    )


def add(*terms):
    total = terms[0].astype(F32)
    for term in terms[1:]:
        total = total + term.astype(F32)
    return total.astype(BF)


def first_hops(start):
    return {
        (0, 0): start,
        (0, 1): other_l(start),
        (3, 0): along_x(start, 1),
        (1, 0): along_x(start, -1),
    }


def other_hops(t):
    t[0, 1], t[3, 0], t[1, 0] = lax.optimization_barrier((t[0, 1], t[3, 0], t[1, 0]))
    t[1, 1] = along_x(t[0, 1], -1)
    t[3, 1] = other_l(t[3, 0])
    t[2, 0] = along_x(t[3, 0], 1)
    t[2, 1] = along_x(t[1, 1], -1)


def reduced(q):
    f21 = along_x(q[2, 1], 1)
    f20 = along_x(q[2, 0], -1)
    f31 = other_l(q[3, 1])
    q10, f21 = lax.optimization_barrier((q[1, 0], f21))
    f10 = along_x(q10, 1)
    f11 = along_x(add(q[1, 1], f21), 1)
    f30 = along_x(add(q[3, 0], f20, f31), -1)
    f01 = other_l(add(q[0, 1], f11))
    return [q[0, 0], f10, f30, f01]


def shards(tokens, expert_ids, gates, grad_mixed, w_gate, w_up, w_down):
    tok, width = tokens.shape
    half = width // 2
    ids_t = expert_ids.T
    gates_t = gates.T

    near_own, far_own, near_other, far_other, w_send = whole(
        functools.partial(dispatch_kernel, half),
        [shape(16, half)] * 4 + [shape(3 * half, w_gate.shape[2])],
        (ids_t, gates_t, tokens, grad_mixed, w_gate, w_up, w_down),
        [
            pltpu.VMEM((2, tok), jnp.int32),
            pltpu.VMEM((2, tok), F32),
            pltpu.VMEM((2, tok, half), BF),
            pltpu.VMEM((2, tok, half), BF),
            pltpu.SemaphoreType.DMA((2, 2)),
            pltpu.SemaphoreType.DMA((2,)),
            pltpu.SemaphoreType.DMA((2 + half // 256,)),
        ],
        [HBM] * 7,
        BIG,
    )
    near_got = other_core(near_other)
    far_got = [other_y(far_own), other_y_core(far_other)]
    w_got = other_core(w_send)
    msgs = whole(merge_kernel, [shape(16, half)] * 4, (near_own, near_got, *far_got))
    across = along_z(msgs[2], 2)
    msgs = [msgs[0], along_z(msgs[1], 1), across, along_z(msgs[3], 3)]
    part = half // HALVES
    starts = whole(assemble_kernel, [shape(64, part)] * HALVES, msgs)
    gathered = []
    for start in starts:
        if gathered:
            gathered[0][0, 1], start = lax.optimization_barrier((gathered[0][0, 1], start))
        gathered.append(first_hops(start))
    w_own = weights(half, w_got, w_gate, w_up, w_down)
    for t in gathered:
        other_hops(t)

    fdev = w_gate.shape[2]
    parts = []
    for group in (EARLY, LATE):
        parts.append(
            whole(
                functools.partial(first_kernel, half),
                shape(128, 6 * fdev, F32),
                [t[o] for o in group for t in gathered] + [w_own, w_got],
                [pltpu.VMEM((128, half), BF)] * 2,
            )
        )
    parts += [other_core(part) for part in parts]
    q = {}
    for group in (SENT, KEPT):
        res = whole(
            functools.partial(second_kernel, half, group),
            [shape(64, part)] * (len(group) * HALVES),
            parts + [w_own, w_got],
            [pltpu.VMEM((32 * len(group), 2 * fdev), BF)] * 3,
        )
        q.update(zip([(n, *o) for o in group for n in range(HALVES)], res))

    terms = []
    for n in range(HALVES):
        terms += reduced({key[1:]: value for key, value in q.items() if key[0] == n})
    back = whole(finish_kernel, [shape(16, half)] * 4, terms)
    across = along_z(back[2], -2)
    back = [back[0], along_z(back[1], -1), across, along_z(back[3], -3)]
    near_mine, near_theirs, far_mine, far_theirs = whole(cores_kernel, [shape(16, half)] * 4, back)
    outs = [shape(tok, width), shape(tok, width)]
    scratch = [pltpu.VMEM((tok, half), BF), pltpu.VMEM((tok, half), BF), pltpu.SemaphoreType.DMA((2,))]
    rest = (ids_t, gates_t, tokens, grad_mixed)
    mixed, grad_tokens, inner = pl.pallas_call(
        functools.partial(tail_kernel, half, False),
        out_shape=outs + [shape(16, 128, F32)],
        in_specs=[VMEM] * 6,
        out_specs=[HBM, HBM, VMEM],
        scratch_shapes=scratch,
        compiler_params=pltpu.CompilerParams(vmem_limit_bytes=LIMIT),
    )(*rest, near_mine, other_y(far_mine))
    mixed, grad_tokens, grad_gates = pl.pallas_call(
        functools.partial(tail_kernel, half, True),
        out_shape=outs + [shape(2, tok, F32)],
        in_specs=[VMEM] * 7 + [HBM, HBM],
        out_specs=[HBM, HBM, VMEM],
        input_output_aliases={7: 0, 8: 1},
        scratch_shapes=scratch,
        compiler_params=pltpu.CompilerParams(vmem_limit_bytes=LIMIT),
    )(*rest, other_core(near_theirs), other_y_core(far_theirs), inner, mixed, grad_tokens)
    return mixed, grad_tokens, grad_gates.T


def solution(mesh):
    return jax.shard_map(
        shards,
        mesh=mesh,
        in_specs=(
            P(("dp", "expert"), None),
            P(("dp", "expert"), None),
            P(("dp", "expert"), None),
            P(("dp", "expert"), None),
            P("expert", None, "dp"),
            P("expert", None, "dp"),
            P("expert", "dp", None),
        ),
        out_specs=(P(("dp", "expert"), None), P(("dp", "expert"), None), P(("dp", "expert"), None)),
        check_vma=False,
    )
```

```python
import functools

import jax
import jax.numpy as jnp
from jax import lax
from jax.experimental import pallas as pl
from jax.experimental.pallas import tpu as pltpu
from jax.sharding import PartitionSpec as P

BF = jnp.bfloat16
F32 = jnp.float32
VMEM = pl.BlockSpec(memory_space=pltpu.VMEM)
HBM = pl.BlockSpec(memory_space=pltpu.HBM)
LIMIT = 16 * 1024 * 1024
BIG = 52 * 1024 * 1024
NZ = 4
HALVES = 2


def dot(a, b, dims):
    return lax.dot_general(a, b, (dims, ((), ())), preferred_element_type=F32)


def place_of(index):
    return index // 8, (index // 4) % 2, (index // 2) % 2, index % 2


def index_of(z, h, l, c):
    return ((z * 2 + h) * 2 + l) * 2 + c


def over_expert(value, move):
    pairs = []
    for at in range(32):
        pairs.append((at, index_of(*move(*place_of(at)))))
    return lax.ppermute(value, "expert", pairs)


def other_core(value):
    return over_expert(value, lambda z, h, l, c: (z, h, l, 1 - c))


def other_l(value):
    return over_expert(value, lambda z, h, l, c: (z, h, 1 - l, c))


def other_y(value):
    return over_expert(value, lambda z, h, l, c: (z, 1 - h, 1 - l, c))


def other_y_core(value):
    return over_expert(value, lambda z, h, l, c: (z, 1 - h, 1 - l, 1 - c))


def along_z(value, step):
    return over_expert(value, lambda z, h, l, c: ((z + step) % NZ, h, l, c))


def along_x(value, step):
    pairs = []
    for x in range(4):
        for at in range(32):
            to = (x + step) % 4 if at % 2 == 0 else (x - step) % 4
            pairs.append((x * 32 + at, to * 32 + at))
    return lax.ppermute(value, ("dp", "expert"), pairs)


def selection(ids, rows, expert, place):
    tok = ids.shape[1]
    up = (lax.broadcasted_iota(jnp.int32, (tok, tok), 0) < lax.broadcasted_iota(jnp.int32, (tok, tok), 1))
    up = jnp.where(up, 1.0, 0.0).astype(BF)
    first = jnp.where(jnp.broadcast_to(ids[0:1, :], (rows, tok)) == expert, 1.0, 0.0)
    second = jnp.where(jnp.broadcast_to(ids[1:2, :], (rows, tok)) == expert, 1.0, 0.0)
    before_first = dot(first.astype(BF), up, ((1,), (0,)))
    before_second = dot(second.astype(BF), up, ((1,), (0,))) + jnp.sum(first, axis=1, keepdims=True)
    want = place.astype(F32)
    sel_first = jnp.where(before_first == want, first, 0.0)
    sel_second = jnp.where(before_second == want, second, 0.0)
    return sel_first, sel_second


def slot_expert(k, r, z, h):
    return ((z + k) & 3) * 2 + ((h + r) & 1)


def weight_copies(half, core, wg_ref, wu_ref, wd_ref, out_ref, sems):
    at = core * half
    rows = pl.ds(pl.multiple_of(at, 256), half)
    copies = [
        pltpu.make_async_copy(wg_ref.at[0, rows, :], out_ref.at[pl.ds(0, half), :], sems.at[0]),
        pltpu.make_async_copy(wu_ref.at[0, rows, :], out_ref.at[pl.ds(half, half), :], sems.at[1]),
    ]
    for n in range(half // 256):
        cols = pl.ds(pl.multiple_of(at + 256 * n, 256), 256)
        into = out_ref.at[pl.ds(2 * half + 256 * n, 256), :]
        copies.append(pltpu.make_async_copy(wd_ref.at[0, :, cols], into, sems.at[2 + n]))
    for copy in copies:
        copy.start()
    return copies


def weights_kernel(half, after_ref, wg_ref, wu_ref, wd_ref, out_ref, sems):
    core = lax.axis_index("expert") & 1
    for copy in weight_copies(half, core, wg_ref, wu_ref, wd_ref, out_ref, sems):
        copy.wait()


def dispatch_kernel(
    half,
    ids_hbm,
    gates_hbm,
    tok_hbm,
    grad_hbm,
    wg_hbm,
    wu_hbm,
    wd_hbm,
    near_own,
    far_own,
    near_other,
    far_other,
    w_send,
    ids_ref,
    gates_ref,
    tok_v,
    grad_v,
    sems,
    small,
    w_sems,
):
    few = [
        pltpu.make_async_copy(ids_hbm, ids_ref, small.at[0]),
        pltpu.make_async_copy(gates_hbm, gates_ref, small.at[1]),
    ]
    for copy in few:
        copy.start()
    at = lax.axis_index("expert")
    core = at & 1
    h = (at >> 2) & 1
    z = at >> 3
    copies = []
    for n, which in enumerate((1 - core, core)):
        cols = pl.ds(pl.multiple_of(which * half, 128), half)
        one = pltpu.make_async_copy(tok_hbm.at[:, cols], tok_v.at[n], sems.at[n, 0])
        two = pltpu.make_async_copy(grad_hbm.at[:, cols], grad_v.at[n], sems.at[n, 1])
        one.start()
        two.start()
        copies.append((one, two))
    big = weight_copies(half, 1 - core, wg_hbm, wu_hbm, wd_hbm, w_send, w_sems)
    for copy in few:
        copy.wait()
    rows, tok = 32, ids_ref.shape[1]
    s = lax.broadcasted_iota(jnp.int32, (rows, tok), 0)
    sel_first, sel_second = selection(ids_ref[...], rows, slot_expert((s >> 1) & 3, s >> 4, z, h), s & 1)
    is_grad = ((s >> 3) & 1) == 1
    member = sel_first + sel_second
    gate = jnp.sum(
        sel_first * jnp.broadcast_to(gates_ref[0:1, :], (rows, tok))
        + sel_second * jnp.broadcast_to(gates_ref[1:2, :], (rows, tok)),
        axis=1,
        keepdims=True,
    )
    of_tok = jnp.where(is_grad, 0.0, member).astype(BF)
    of_grad = jnp.where(is_grad, member, 0.0).astype(BF)
    for n, (near, far) in enumerate(((near_other, far_other), (near_own, far_own))):
        copies[n][0].wait()
        copies[n][1].wait()
        got = dot(of_tok, tok_v[n], ((1,), (0,))) + dot(of_grad, grad_v[n], ((1,), (0,))) * gate
        got = got.astype(BF)
        near[...] = got[0:16, :]
        far[...] = got[16:32, :]
    for copy in big:
        copy.wait()


def merge_kernel(near_own, near_got, far_own, far_got, *outs):
    core = lax.axis_index("expert") & 1
    full = jnp.concatenate([near_own[...], near_got[...], far_own[...], far_got[...]], axis=0)
    s = lax.broadcasted_iota(jnp.int32, (64, 64), 0)
    t = lax.broadcasted_iota(jnp.int32, (64, 64), 1)
    k, kind, r, c, j = s >> 4, (s >> 3) & 1, (s >> 2) & 1, (s >> 1) & 1, s & 1
    source = r * 32 + ((c + core) & 1) * 16 + kind * 8 + k * 2 + j
    both = dot(jnp.where(t == source, 1.0, 0.0).astype(BF), full, ((1,), (0,))).astype(BF)
    for n, out in enumerate(outs):
        out[...] = both[16 * n : 16 * n + 16, :]


def assemble_kernel(m0, m1, m2, m3, *outs):
    wide = [m[...].astype(F32) for m in (m0, m1, m2, m3)]
    full = jnp.concatenate([m[0:8] for m in wide] + [m[8:16] for m in wide], axis=0).astype(BF)
    part = full.shape[1] // len(outs)
    for n, out in enumerate(outs):
        out[...] = full[:, part * n : part * n + part]


def first_kernel(half, *refs):
    chunks, (own, got, out, rows, grads) = refs[:-5], refs[-5:]
    part = chunks[0].shape[1]
    for n, chunk in enumerate(chunks):
        at, cols = pl.ds(32 * (n // HALVES), 32), pl.ds(part * (n % HALVES), part)
        rows[at, cols] = chunk[0:32, :]
        grads[at, cols] = chunk[32:64, :]
    for m, w in enumerate((own, got)):
        at = 256 * m
        out[:, at : at + 256] = dot(rows[...], w[0:half, :], ((1,), (0,)))
        out[:, 512 + at : 768 + at] = dot(rows[...], w[half : 2 * half, :], ((1,), (0,)))
        last = dot(grads[:, 0:256], w[2 * half : 2 * half + 256, :], ((1,), (1,)))
        for n in range(1, half // 256):
            block = w[2 * half + 256 * n : 2 * half + 256 * n + 256, :]
            last += dot(grads[:, 256 * n : 256 * n + 256], block, ((1,), (1,)))
        out[:, 1024 + at : 1280 + at] = last


EARLY = [(0, 0), (3, 0), (1, 0), (0, 1)]
LATE = [(1, 1), (3, 1), (2, 0), (2, 1)]
SENT = [(2, 1), (2, 0), (3, 1), (1, 0)]
KEPT = [(1, 1), (3, 0), (0, 1), (0, 0)]


def second_kernel(half, chunks, *refs):
    parts, (own, got) = refs[:4], refs[4:6]
    outs, (hid_ref, ga_ref, gb_ref) = refs[6:-3], refs[-3:]
    for n, (a_at, b_at) in enumerate(chunks):
        late = (a_at, b_at) in LATE
        mine, theirs = parts[1 if late else 0], parts[3 if late else 2]
        group = LATE if late else EARLY
        here = pl.ds(32 * group.index((a_at, b_at)), 32)
        there = pl.ds(32 * group.index(((-a_at) % 4, b_at)), 32)

        def both(base):
            return jnp.concatenate(
                [
                    mine[here, base : base + 256] + theirs[there, base + 256 : base + 512],
                    mine[here, base + 256 : base + 512] + theirs[there, base : base + 256],
                ],
                axis=1,
            )

        a, b, gh = both(0), both(512), both(1024)
        sg = jax.nn.sigmoid(a)
        at = pl.ds(32 * n, 32)
        hid_ref[at, :] = (a * sg * b).astype(BF)
        ga_ref[at, :] = (gh * b * sg * (1.0 + a * (1.0 - sg))).astype(BF)
        gb_ref[at, :] = (gh * a * sg).astype(BF)

    for n in range(half // 256):
        at = 256 * n
        res, gres = None, None
        for m, w in enumerate((own, got)):
            cols = slice(256 * m, 256 * m + 256)
            one = dot(hid_ref[:, cols], w[2 * half + at : 2 * half + at + 256, :], ((1,), (0,)))
            two = dot(ga_ref[:, cols], w[at : at + 256, :], ((1,), (1,)))
            two += dot(gb_ref[:, cols], w[half + at : half + at + 256, :], ((1,), (1,)))
            res = one if res is None else res + one
            gres = two if gres is None else gres + two
        res, gres = res.astype(BF), gres.astype(BF)
        part = half // HALVES
        for k in range(len(chunks)):
            out = outs[HALVES * k + at // part]
            into = at % part
            out[0:32, into : into + 256] = res[32 * k : 32 * k + 32, :]
            out[32:64, into : into + 256] = gres[32 * k : 32 * k + 32, :]


def finish_kernel(*refs):
    terms, outs = refs[:-4], refs[-4:]
    totals = []
    for n in range(HALVES):
        total = terms[4 * n][...].astype(F32)
        for ref in terms[4 * n + 1 : 4 * n + 4]:
            total += ref[...].astype(F32)
        totals.append(total)
    total = jnp.concatenate(totals, axis=1)
    for k, out in enumerate(outs):
        out[...] = jnp.concatenate([total[8 * k : 8 * k + 8], total[32 + 8 * k : 40 + 8 * k]], axis=0).astype(BF)


def cores_kernel(*refs):
    msgs, outs = refs[:4], refs[4:]
    core = lax.axis_index("expert") & 1
    full = jnp.concatenate([m[...] for m in msgs], axis=0)
    s = lax.broadcasted_iota(jnp.int32, (64, 64), 0)
    t = lax.broadcasted_iota(jnp.int32, (64, 64), 1)
    r, c, kind, k, j = s >> 5, (s >> 4) & 1, (s >> 3) & 1, (s >> 1) & 3, s & 1
    source = k * 16 + kind * 8 + r * 4 + ((c + core) & 1) * 2 + j
    both = dot(jnp.where(t == source, 1.0, 0.0).astype(BF), full, ((1,), (0,))).astype(BF)
    for n, out in enumerate(outs):
        out[...] = both[16 * n : 16 * n + 16, :]


def tail_kernel(half, other, ids_ref, gates_ref, tok_ref, grad_ref, near, far, *refs):
    if other:
        inner_ref, _, _, mixed_hbm, gt_hbm, gg_ref, mixed_ref, gt_ref, sems = refs
    else:
        mixed_hbm, gt_hbm, inner_ref, mixed_ref, gt_ref, sems = refs
    at = lax.axis_index("expert")
    core = at & 1
    which = 1 - core if other else core
    rows, tok = 16, ids_ref.shape[1]
    s = lax.broadcasted_iota(jnp.int32, (rows, tok), 0)
    expert = slot_expert((s >> 1) & 3, s >> 3, at >> 3, (at >> 2) & 1)
    sel_first, sel_second = selection(ids_ref[...], rows, expert, s & 1)
    member = (sel_first + sel_second).astype(BF)
    gate = jnp.sum(
        sel_first * jnp.broadcast_to(gates_ref[0:1, :], (rows, tok))
        + sel_second * jnp.broadcast_to(gates_ref[1:2, :], (rows, tok)),
        axis=1,
        keepdims=True,
    )
    cols = pl.ds(pl.multiple_of(which * half, 128), half)
    one, two = near[...].astype(F32), far[...].astype(F32)
    out_rows = jnp.concatenate([one[0:8], two[0:8]], axis=0)
    grad_rows = jnp.concatenate([one[8:16], two[8:16]], axis=0).astype(BF)
    grad = grad_ref[:, cols]
    gt_ref[...] = (grad.astype(F32) + dot(member, grad_rows, ((0,), (0,)))).astype(BF)
    first = pltpu.make_async_copy(gt_ref, gt_hbm.at[:, cols], sems.at[0])
    first.start()
    scaled = out_rows * gate
    high = scaled.astype(BF)
    low = (scaled - high.astype(F32)).astype(BF)
    add = dot(member, high, ((0,), (0,))) + dot(member, low, ((0,), (0,)))
    mixed_ref[...] = (tok_ref[:, cols].astype(F32) + add).astype(BF)
    second = pltpu.make_async_copy(mixed_ref, mixed_hbm.at[:, cols], sems.at[1])
    second.start()
    inner = jnp.sum(dot(member, grad, ((1,), (0,))) * out_rows, axis=1, keepdims=True)
    if other:
        inner += inner_ref[:, 0:1]
        gg_ref[0:1, :] = jnp.sum(sel_first * inner, axis=0, keepdims=True)
        gg_ref[1:2, :] = jnp.sum(sel_second * inner, axis=0, keepdims=True)
    else:
        inner_ref[...] = jnp.broadcast_to(inner, inner_ref.shape)
    first.wait()
    second.wait()


def shape(rows, cols, dtype=BF):
    return jax.ShapeDtypeStruct((rows, cols), dtype)


def whole(kernel, outs, args, scratch=(), specs=None, limit=LIMIT):
    return pl.pallas_call(
        kernel,
        out_shape=outs,
        in_specs=specs or [VMEM] * len(args),
        out_specs=jax.tree.map(lambda _: VMEM, outs),
        scratch_shapes=list(scratch),
        compiler_params=pltpu.CompilerParams(vmem_limit_bytes=limit),
    )(*args)


def weights(half, after, w_gate, w_up, w_down):
    return whole(
        functools.partial(weights_kernel, half),
        shape(3 * half, w_gate.shape[2]),
        (after, w_gate, w_up, w_down),
        [pltpu.SemaphoreType.DMA((2 + half // 256,))],
        [HBM] * 4,
    )


def add(*terms):
    total = terms[0].astype(F32)
    for term in terms[1:]:
        total = total + term.astype(F32)
    return total.astype(BF)


def first_hops(start):
    return {
        (0, 0): start,
        (0, 1): other_l(start),
        (3, 0): along_x(start, 1),
        (1, 0): along_x(start, -1),
    }


def other_hops(t):
    t[0, 1], t[3, 0], t[1, 0] = lax.optimization_barrier((t[0, 1], t[3, 0], t[1, 0]))
    t[1, 1] = along_x(t[0, 1], -1)
    t[3, 1] = other_l(t[3, 0])
    t[2, 0] = along_x(t[3, 0], 1)
    t[2, 1] = along_x(t[1, 1], -1)


def reduced(q):
    f21 = along_x(q[2, 1], 1)
    f20 = along_x(q[2, 0], -1)
    f31 = other_l(q[3, 1])
    f11 = along_x(add(q[1, 1], f21), 1)
    f30 = along_x(add(q[3, 0], f20, f31), -1)
    q10, f11 = lax.optimization_barrier((q[1, 0], f11))
    f01 = other_l(add(q[0, 1], f11))
    f10 = along_x(q10, 1)
    return [q[0, 0], f10, f30, f01]


def shards(tokens, expert_ids, gates, grad_mixed, w_gate, w_up, w_down):
    tok, width = tokens.shape
    half = width // 2
    ids_t = expert_ids.T
    gates_t = gates.T

    near_own, far_own, near_other, far_other, w_send = whole(
        functools.partial(dispatch_kernel, half),
        [pltpu.VMEM((16, half), BF)] * 4 + [pltpu.VMEM((3 * half, w_gate.shape[2]), BF)],
        (ids_t, gates_t, tokens, grad_mixed, w_gate, w_up, w_down),
        [
            pltpu.VMEM((2, tok), jnp.int32),
            pltpu.VMEM((2, tok), F32),
            pltpu.VMEM((2, tok, half), BF),
            pltpu.VMEM((2, tok, half), BF),
            pltpu.SemaphoreType.DMA((2, 2)),
            pltpu.SemaphoreType.DMA((2,)),
            pltpu.SemaphoreType.DMA((2 + half // 256,)),
        ],
        [HBM] * 7,
        BIG,
    )
    near_got = other_core(near_other)
    far_got = [other_y(far_own), other_y_core(far_other)]
    w_got = other_core(w_send)
    msgs = whole(merge_kernel, [shape(16, half)] * 4, (near_own, near_got, *far_got))
    across = along_z(msgs[2], 2)
    msgs = [msgs[0], along_z(msgs[1], 1), across, along_z(msgs[3], 3)]
    part = half // HALVES
    starts = whole(assemble_kernel, [shape(64, part)] * HALVES, msgs)
    gathered = []
    for start in starts:
        if gathered:
            gathered[0][0, 1], start = lax.optimization_barrier((gathered[0][0, 1], start))
        gathered.append(first_hops(start))
    w_own = weights(half, w_got, w_gate, w_up, w_down)
    for t in gathered:
        other_hops(t)

    fdev = w_gate.shape[2]
    parts = []
    for group in (EARLY, LATE):
        parts.append(
            whole(
                functools.partial(first_kernel, half),
                shape(128, 6 * fdev, F32),
                [t[o] for o in group for t in gathered] + [w_own, w_got],
                [pltpu.VMEM((128, half), BF)] * 2,
            )
        )
    parts += [other_core(part) for part in parts]
    q = {}
    for group in (SENT, KEPT):
        res = whole(
            functools.partial(second_kernel, half, group),
            [shape(64, part)] * (len(group) * HALVES),
            parts + [w_own, w_got],
            [pltpu.VMEM((32 * len(group), 2 * fdev), BF)] * 3,
        )
        q.update(zip([(n, *o) for o in group for n in range(HALVES)], res))

    terms = []
    for n in range(HALVES):
        terms += reduced({key[1:]: value for key, value in q.items() if key[0] == n})
    back = whole(finish_kernel, [shape(16, half)] * 4, terms)
    across = along_z(back[2], -2)
    back = [back[0], along_z(back[1], -1), across, along_z(back[3], -3)]
    near_mine, near_theirs, far_mine, far_theirs = whole(cores_kernel, [shape(16, half)] * 4, back)
    outs = [shape(tok, width), shape(tok, width)]
    scratch = [pltpu.VMEM((tok, half), BF), pltpu.VMEM((tok, half), BF), pltpu.SemaphoreType.DMA((2,))]
    rest = (ids_t, gates_t, tokens, grad_mixed)
    mixed, grad_tokens, inner = pl.pallas_call(
        functools.partial(tail_kernel, half, False),
        out_shape=outs + [shape(16, 128, F32)],
        in_specs=[VMEM] * 6,
        out_specs=[HBM, HBM, VMEM],
        scratch_shapes=scratch,
        compiler_params=pltpu.CompilerParams(vmem_limit_bytes=LIMIT),
    )(*rest, near_mine, other_y(far_mine))
    mixed, grad_tokens, grad_gates = pl.pallas_call(
        functools.partial(tail_kernel, half, True),
        out_shape=outs + [shape(2, tok, F32)],
        in_specs=[VMEM] * 7 + [HBM, HBM],
        out_specs=[HBM, HBM, VMEM],
        input_output_aliases={7: 0, 8: 1},
        scratch_shapes=scratch,
        compiler_params=pltpu.CompilerParams(vmem_limit_bytes=LIMIT),
    )(*rest, other_core(near_theirs), other_y_core(far_theirs), inner, mixed, grad_tokens)
    return mixed, grad_tokens, grad_gates.T


def solution(mesh):
    return jax.shard_map(
        shards,
        mesh=mesh,
        in_specs=(
            P(("dp", "expert"), None),
            P(("dp", "expert"), None),
            P(("dp", "expert"), None),
            P(("dp", "expert"), None),
            P("expert", None, "dp"),
            P("expert", None, "dp"),
            P("expert", "dp", None),
        ),
        out_specs=(P(("dp", "expert"), None), P(("dp", "expert"), None), P(("dp", "expert"), None)),
        check_vma=False,
    )
```

```python
import functools

import jax
import jax.numpy as jnp
from jax import lax
from jax.experimental import pallas as pl
from jax.experimental.pallas import tpu as pltpu
from jax.sharding import PartitionSpec as P

BF = jnp.bfloat16
F32 = jnp.float32
VMEM = pl.BlockSpec(memory_space=pltpu.VMEM)
HBM = pl.BlockSpec(memory_space=pltpu.HBM)
LIMIT = 16 * 1024 * 1024
BIG = 52 * 1024 * 1024
NZ = 4
HALVES = 2


def dot(a, b, dims):
    return lax.dot_general(a, b, (dims, ((), ())), preferred_element_type=F32)


def place_of(index):
    return index // 8, (index // 4) % 2, (index // 2) % 2, index % 2


def index_of(z, h, l, c):
    return ((z * 2 + h) * 2 + l) * 2 + c


def over_expert(value, move):
    pairs = []
    for at in range(32):
        pairs.append((at, index_of(*move(*place_of(at)))))
    return lax.ppermute(value, "expert", pairs)


def other_core(value):
    return over_expert(value, lambda z, h, l, c: (z, h, l, 1 - c))


def other_l(value):
    return over_expert(value, lambda z, h, l, c: (z, h, 1 - l, c))


def other_y(value):
    return over_expert(value, lambda z, h, l, c: (z, 1 - h, 1 - l, c))


def other_y_core(value):
    return over_expert(value, lambda z, h, l, c: (z, 1 - h, 1 - l, 1 - c))


def along_z(value, step):
    return over_expert(value, lambda z, h, l, c: ((z + step) % NZ, h, l, c))


def along_x(value, step):
    pairs = []
    for x in range(4):
        for at in range(32):
            to = (x + step) % 4 if at % 2 == 0 else (x - step) % 4
            pairs.append((x * 32 + at, to * 32 + at))
    return lax.ppermute(value, ("dp", "expert"), pairs)


def selection(ids, rows, expert, place):
    tok = ids.shape[1]
    up = (lax.broadcasted_iota(jnp.int32, (tok, tok), 0) < lax.broadcasted_iota(jnp.int32, (tok, tok), 1))
    up = jnp.where(up, 1.0, 0.0).astype(BF)
    first = jnp.where(jnp.broadcast_to(ids[0:1, :], (rows, tok)) == expert, 1.0, 0.0)
    second = jnp.where(jnp.broadcast_to(ids[1:2, :], (rows, tok)) == expert, 1.0, 0.0)
    before_first = dot(first.astype(BF), up, ((1,), (0,)))
    before_second = dot(second.astype(BF), up, ((1,), (0,))) + jnp.sum(first, axis=1, keepdims=True)
    want = place.astype(F32)
    sel_first = jnp.where(before_first == want, first, 0.0)
    sel_second = jnp.where(before_second == want, second, 0.0)
    return sel_first, sel_second


def slot_expert(k, r, z, h):
    return ((z + k) & 3) * 2 + ((h + r) & 1)


def weight_copies(half, core, wg_ref, wu_ref, wd_ref, out_ref, sems):
    at = core * half
    rows = pl.ds(pl.multiple_of(at, 256), half)
    copies = [
        pltpu.make_async_copy(wg_ref.at[0, rows, :], out_ref.at[pl.ds(0, half), :], sems.at[0]),
        pltpu.make_async_copy(wu_ref.at[0, rows, :], out_ref.at[pl.ds(half, half), :], sems.at[1]),
    ]
    for n in range(half // 256):
        cols = pl.ds(pl.multiple_of(at + 256 * n, 256), 256)
        into = out_ref.at[pl.ds(2 * half + 256 * n, 256), :]
        copies.append(pltpu.make_async_copy(wd_ref.at[0, :, cols], into, sems.at[2 + n]))
    for copy in copies:
        copy.start()
    return copies


def weights_kernel(half, after_ref, wg_ref, wu_ref, wd_ref, out_ref, sems):
    core = lax.axis_index("expert") & 1
    for copy in weight_copies(half, core, wg_ref, wu_ref, wd_ref, out_ref, sems):
        copy.wait()


def dispatch_kernel(
    half,
    ids_hbm,
    gates_hbm,
    tok_hbm,
    grad_hbm,
    wg_hbm,
    wu_hbm,
    wd_hbm,
    near_own,
    far_own,
    near_other,
    far_other,
    w_send,
    ids_ref,
    gates_ref,
    tok_v,
    grad_v,
    sems,
    small,
    w_sems,
):
    few = [
        pltpu.make_async_copy(ids_hbm, ids_ref, small.at[0]),
        pltpu.make_async_copy(gates_hbm, gates_ref, small.at[1]),
    ]
    for copy in few:
        copy.start()
    at = lax.axis_index("expert")
    core = at & 1
    h = (at >> 2) & 1
    z = at >> 3
    copies = []
    for n, which in enumerate((1 - core, core)):
        cols = pl.ds(pl.multiple_of(which * half, 128), half)
        one = pltpu.make_async_copy(tok_hbm.at[:, cols], tok_v.at[n], sems.at[n, 0])
        two = pltpu.make_async_copy(grad_hbm.at[:, cols], grad_v.at[n], sems.at[n, 1])
        one.start()
        two.start()
        copies.append((one, two))
    big = weight_copies(half, 1 - core, wg_hbm, wu_hbm, wd_hbm, w_send, w_sems)
    for copy in few:
        copy.wait()
    rows, tok = 32, ids_ref.shape[1]
    s = lax.broadcasted_iota(jnp.int32, (rows, tok), 0)
    sel_first, sel_second = selection(ids_ref[...], rows, slot_expert((s >> 1) & 3, s >> 4, z, h), s & 1)
    is_grad = ((s >> 3) & 1) == 1
    member = sel_first + sel_second
    gate = jnp.sum(
        sel_first * jnp.broadcast_to(gates_ref[0:1, :], (rows, tok))
        + sel_second * jnp.broadcast_to(gates_ref[1:2, :], (rows, tok)),
        axis=1,
        keepdims=True,
    )
    of_tok = jnp.where(is_grad, 0.0, member).astype(BF)
    of_grad = jnp.where(is_grad, member, 0.0).astype(BF)
    for n, (near, far) in enumerate(((near_other, far_other), (near_own, far_own))):
        copies[n][0].wait()
        copies[n][1].wait()
        got = dot(of_tok, tok_v[n], ((1,), (0,))) + dot(of_grad, grad_v[n], ((1,), (0,))) * gate
        got = got.astype(BF)
        near[...] = got[0:16, :]
        far[...] = got[16:32, :]
    for copy in big:
        copy.wait()


def merge_kernel(near_own, near_got, far_own, far_got, *outs):
    core = lax.axis_index("expert") & 1
    full = jnp.concatenate([near_own[...], near_got[...], far_own[...], far_got[...]], axis=0)
    s = lax.broadcasted_iota(jnp.int32, (64, 64), 0)
    t = lax.broadcasted_iota(jnp.int32, (64, 64), 1)
    k, kind, r, c, j = s >> 4, (s >> 3) & 1, (s >> 2) & 1, (s >> 1) & 1, s & 1
    source = r * 32 + ((c + core) & 1) * 16 + kind * 8 + k * 2 + j
    both = dot(jnp.where(t == source, 1.0, 0.0).astype(BF), full, ((1,), (0,))).astype(BF)
    for n, out in enumerate(outs):
        out[...] = both[16 * n : 16 * n + 16, :]


def assemble_kernel(m0, m1, m2, m3, *outs):
    wide = [m[...].astype(F32) for m in (m0, m1, m2, m3)]
    full = jnp.concatenate([m[0:8] for m in wide] + [m[8:16] for m in wide], axis=0).astype(BF)
    part = full.shape[1] // len(outs)
    for n, out in enumerate(outs):
        out[...] = full[:, part * n : part * n + part]


def first_kernel(half, *refs):
    chunks, (own, got, out, rows, grads) = refs[:-5], refs[-5:]
    part = chunks[0].shape[1]
    for n, chunk in enumerate(chunks):
        at, cols = pl.ds(32 * (n // HALVES), 32), pl.ds(part * (n % HALVES), part)
        rows[at, cols] = chunk[0:32, :]
        grads[at, cols] = chunk[32:64, :]
    for m, w in enumerate((own, got)):
        at = 256 * m
        out[:, at : at + 256] = dot(rows[...], w[0:half, :], ((1,), (0,)))
        out[:, 512 + at : 768 + at] = dot(rows[...], w[half : 2 * half, :], ((1,), (0,)))
        last = dot(grads[:, 0:256], w[2 * half : 2 * half + 256, :], ((1,), (1,)))
        for n in range(1, half // 256):
            block = w[2 * half + 256 * n : 2 * half + 256 * n + 256, :]
            last += dot(grads[:, 256 * n : 256 * n + 256], block, ((1,), (1,)))
        out[:, 1024 + at : 1280 + at] = last


EARLY = [(0, 0), (3, 0), (1, 0), (0, 1)]
LATE = [(1, 1), (3, 1), (2, 0), (2, 1)]
SENT = [(2, 1), (2, 0), (3, 1)]
KEPT = [(1, 1), (3, 0), (0, 1), (1, 0), (0, 0)]


def second_kernel(half, chunks, *refs):
    parts, (own, got) = refs[:4], refs[4:6]
    outs, (hid_ref, ga_ref, gb_ref) = refs[6:-3], refs[-3:]
    for n, (a_at, b_at) in enumerate(chunks):
        late = (a_at, b_at) in LATE
        mine, theirs = parts[1 if late else 0], parts[3 if late else 2]
        group = LATE if late else EARLY
        here = pl.ds(32 * group.index((a_at, b_at)), 32)
        there = pl.ds(32 * group.index(((-a_at) % 4, b_at)), 32)

        def both(base):
            return jnp.concatenate(
                [
                    mine[here, base : base + 256] + theirs[there, base + 256 : base + 512],
                    mine[here, base + 256 : base + 512] + theirs[there, base : base + 256],
                ],
                axis=1,
            )

        a, b, gh = both(0), both(512), both(1024)
        sg = jax.nn.sigmoid(a)
        at = pl.ds(32 * n, 32)
        hid_ref[at, :] = (a * sg * b).astype(BF)
        ga_ref[at, :] = (gh * b * sg * (1.0 + a * (1.0 - sg))).astype(BF)
        gb_ref[at, :] = (gh * a * sg).astype(BF)

    for n in range(half // 256):
        at = 256 * n
        res, gres = None, None
        for m, w in enumerate((own, got)):
            cols = slice(256 * m, 256 * m + 256)
            one = dot(hid_ref[:, cols], w[2 * half + at : 2 * half + at + 256, :], ((1,), (0,)))
            two = dot(ga_ref[:, cols], w[at : at + 256, :], ((1,), (1,)))
            two += dot(gb_ref[:, cols], w[half + at : half + at + 256, :], ((1,), (1,)))
            res = one if res is None else res + one
            gres = two if gres is None else gres + two
        res, gres = res.astype(BF), gres.astype(BF)
        part = half // HALVES
        for k in range(len(chunks)):
            out = outs[HALVES * k + at // part]
            into = at % part
            out[0:32, into : into + 256] = res[32 * k : 32 * k + 32, :]
            out[32:64, into : into + 256] = gres[32 * k : 32 * k + 32, :]


def finish_kernel(*refs):
    terms, outs = refs[:-4], refs[-4:]
    totals = []
    for n in range(HALVES):
        total = terms[4 * n][...].astype(F32)
        for ref in terms[4 * n + 1 : 4 * n + 4]:
            total += ref[...].astype(F32)
        totals.append(total)
    total = jnp.concatenate(totals, axis=1)
    for k, out in enumerate(outs):
        out[...] = jnp.concatenate([total[8 * k : 8 * k + 8], total[32 + 8 * k : 40 + 8 * k]], axis=0).astype(BF)


def cores_kernel(*refs):
    msgs, outs = refs[:4], refs[4:]
    core = lax.axis_index("expert") & 1
    full = jnp.concatenate([m[...] for m in msgs], axis=0)
    s = lax.broadcasted_iota(jnp.int32, (64, 64), 0)
    t = lax.broadcasted_iota(jnp.int32, (64, 64), 1)
    r, c, kind, k, j = s >> 5, (s >> 4) & 1, (s >> 3) & 1, (s >> 1) & 3, s & 1
    source = k * 16 + kind * 8 + r * 4 + ((c + core) & 1) * 2 + j
    both = dot(jnp.where(t == source, 1.0, 0.0).astype(BF), full, ((1,), (0,))).astype(BF)
    for n, out in enumerate(outs):
        out[...] = both[16 * n : 16 * n + 16, :]


def tail_kernel(half, other, ids_ref, gates_ref, tok_ref, grad_ref, near, far, *refs):
    if other:
        inner_ref, _, _, mixed_hbm, gt_hbm, gg_ref, mixed_ref, gt_ref, sems = refs
    else:
        mixed_hbm, gt_hbm, inner_ref, mixed_ref, gt_ref, sems = refs
    at = lax.axis_index("expert")
    core = at & 1
    which = 1 - core if other else core
    rows, tok = 16, ids_ref.shape[1]
    s = lax.broadcasted_iota(jnp.int32, (rows, tok), 0)
    expert = slot_expert((s >> 1) & 3, s >> 3, at >> 3, (at >> 2) & 1)
    sel_first, sel_second = selection(ids_ref[...], rows, expert, s & 1)
    member = (sel_first + sel_second).astype(BF)
    gate = jnp.sum(
        sel_first * jnp.broadcast_to(gates_ref[0:1, :], (rows, tok))
        + sel_second * jnp.broadcast_to(gates_ref[1:2, :], (rows, tok)),
        axis=1,
        keepdims=True,
    )
    cols = pl.ds(pl.multiple_of(which * half, 128), half)
    one, two = near[...].astype(F32), far[...].astype(F32)
    out_rows = jnp.concatenate([one[0:8], two[0:8]], axis=0)
    grad_rows = jnp.concatenate([one[8:16], two[8:16]], axis=0).astype(BF)
    grad = grad_ref[:, cols]
    gt_ref[...] = (grad.astype(F32) + dot(member, grad_rows, ((0,), (0,)))).astype(BF)
    first = pltpu.make_async_copy(gt_ref, gt_hbm.at[:, cols], sems.at[0])
    first.start()
    scaled = out_rows * gate
    high = scaled.astype(BF)
    low = (scaled - high.astype(F32)).astype(BF)
    add = dot(member, high, ((0,), (0,))) + dot(member, low, ((0,), (0,)))
    mixed_ref[...] = (tok_ref[:, cols].astype(F32) + add).astype(BF)
    second = pltpu.make_async_copy(mixed_ref, mixed_hbm.at[:, cols], sems.at[1])
    second.start()
    inner = jnp.sum(dot(member, grad, ((1,), (0,))) * out_rows, axis=1, keepdims=True)
    if other:
        inner += inner_ref[:, 0:1]
        gg_ref[0:1, :] = jnp.sum(sel_first * inner, axis=0, keepdims=True)
        gg_ref[1:2, :] = jnp.sum(sel_second * inner, axis=0, keepdims=True)
    else:
        inner_ref[...] = jnp.broadcast_to(inner, inner_ref.shape)
    first.wait()
    second.wait()


def shape(rows, cols, dtype=BF):
    return jax.ShapeDtypeStruct((rows, cols), dtype)


def whole(kernel, outs, args, scratch=(), specs=None, limit=LIMIT):
    return pl.pallas_call(
        kernel,
        out_shape=outs,
        in_specs=specs or [VMEM] * len(args),
        out_specs=jax.tree.map(lambda _: VMEM, outs),
        scratch_shapes=list(scratch),
        compiler_params=pltpu.CompilerParams(vmem_limit_bytes=limit),
    )(*args)


def weights(half, after, w_gate, w_up, w_down):
    return whole(
        functools.partial(weights_kernel, half),
        shape(3 * half, w_gate.shape[2]),
        (after, w_gate, w_up, w_down),
        [pltpu.SemaphoreType.DMA((2 + half // 256,))],
        [HBM] * 4,
    )


def add(*terms):
    total = terms[0].astype(F32)
    for term in terms[1:]:
        total = total + term.astype(F32)
    return total.astype(BF)


def first_hops(start):
    return {
        (0, 0): start,
        (0, 1): other_l(start),
        (3, 0): along_x(start, 1),
        (1, 0): along_x(start, -1),
    }


def other_hops(t):
    t[0, 1], t[3, 0], t[1, 0] = lax.optimization_barrier((t[0, 1], t[3, 0], t[1, 0]))
    t[1, 1] = along_x(t[0, 1], -1)
    t[3, 1] = other_l(t[3, 0])
    t[2, 0] = along_x(t[3, 0], 1)
    t[2, 1] = along_x(t[1, 1], -1)


def reduced(q):
    f21 = along_x(q[2, 1], 1)
    f20 = along_x(q[2, 0], -1)
    f31 = other_l(q[3, 1])
    f11 = along_x(add(q[1, 1], f21), 1)
    f30 = along_x(add(q[3, 0], f20, f31), -1)
    q10, f11, f30 = lax.optimization_barrier((q[1, 0], f11, f30))
    f01 = other_l(add(q[0, 1], f11))
    f10 = along_x(q10, 1)
    return [q[0, 0], f10, f30, f01]


def shards(tokens, expert_ids, gates, grad_mixed, w_gate, w_up, w_down):
    tok, width = tokens.shape
    half = width // 2
    ids_t = expert_ids.T
    gates_t = gates.T

    near_own, far_own, near_other, far_other, w_send = whole(
        functools.partial(dispatch_kernel, half),
        [pltpu.VMEM((16, half), BF)] * 4 + [pltpu.VMEM((3 * half, w_gate.shape[2]), BF)],
        (ids_t, gates_t, tokens, grad_mixed, w_gate, w_up, w_down),
        [
            pltpu.VMEM((2, tok), jnp.int32),
            pltpu.VMEM((2, tok), F32),
            pltpu.VMEM((2, tok, half), BF),
            pltpu.VMEM((2, tok, half), BF),
            pltpu.SemaphoreType.DMA((2, 2)),
            pltpu.SemaphoreType.DMA((2,)),
            pltpu.SemaphoreType.DMA((2 + half // 256,)),
        ],
        [HBM] * 7,
        BIG,
    )
    near_got = other_core(near_other)
    far_got = [other_y(far_own), other_y_core(far_other)]
    w_got = other_core(w_send)
    msgs = whole(merge_kernel, [shape(16, half)] * 4, (near_own, near_got, *far_got))
    across = along_z(msgs[2], 2)
    msgs = [msgs[0], along_z(msgs[1], 1), across, along_z(msgs[3], 3)]
    part = half // HALVES
    starts = whole(assemble_kernel, [shape(64, part)] * HALVES, msgs)
    gathered = []
    for start in starts:
        if gathered:
            gathered[0][0, 1], start = lax.optimization_barrier((gathered[0][0, 1], start))
        gathered.append(first_hops(start))
    w_own = weights(half, w_got, w_gate, w_up, w_down)
    for t in gathered:
        other_hops(t)

    fdev = w_gate.shape[2]
    parts = []
    for group in (EARLY, LATE):
        parts.append(
            whole(
                functools.partial(first_kernel, half),
                shape(128, 6 * fdev, F32),
                [t[o] for o in group for t in gathered] + [w_own, w_got],
                [pltpu.VMEM((128, half), BF)] * 2,
            )
        )
    parts += [other_core(part) for part in parts]
    q = {}
    for group in (SENT, KEPT):
        res = whole(
            functools.partial(second_kernel, half, group),
            [shape(64, part)] * (len(group) * HALVES),
            parts + [w_own, w_got],
            [pltpu.VMEM((32 * len(group), 2 * fdev), BF)] * 3,
        )
        q.update(zip([(n, *o) for o in group for n in range(HALVES)], res))

    terms = []
    for n in range(HALVES):
        terms += reduced({key[1:]: value for key, value in q.items() if key[0] == n})
    back = whole(finish_kernel, [shape(16, half)] * 4, terms)
    across = along_z(back[2], -2)
    back = [back[0], along_z(back[1], -1), across, along_z(back[3], -3)]
    near_mine, near_theirs, far_mine, far_theirs = whole(cores_kernel, [shape(16, half)] * 4, back)
    outs = [shape(tok, width), shape(tok, width)]
    scratch = [pltpu.VMEM((tok, half), BF), pltpu.VMEM((tok, half), BF), pltpu.SemaphoreType.DMA((2,))]
    rest = (ids_t, gates_t, tokens, grad_mixed)
    mixed, grad_tokens, inner = pl.pallas_call(
        functools.partial(tail_kernel, half, False),
        out_shape=outs + [shape(16, 128, F32)],
        in_specs=[VMEM] * 6,
        out_specs=[HBM, HBM, VMEM],
        scratch_shapes=scratch,
        compiler_params=pltpu.CompilerParams(vmem_limit_bytes=LIMIT),
    )(*rest, near_mine, other_y(far_mine))
    mixed, grad_tokens, grad_gates = pl.pallas_call(
        functools.partial(tail_kernel, half, True),
        out_shape=outs + [shape(2, tok, F32)],
        in_specs=[VMEM] * 7 + [HBM, HBM],
        out_specs=[HBM, HBM, VMEM],
        input_output_aliases={7: 0, 8: 1},
        scratch_shapes=scratch,
        compiler_params=pltpu.CompilerParams(vmem_limit_bytes=LIMIT),
    )(*rest, other_core(near_theirs), other_y_core(far_theirs), inner, mixed, grad_tokens)
    return mixed, grad_tokens, grad_gates.T


def solution(mesh):
    return jax.shard_map(
        shards,
        mesh=mesh,
        in_specs=(
            P(("dp", "expert"), None),
            P(("dp", "expert"), None),
            P(("dp", "expert"), None),
            P(("dp", "expert"), None),
            P("expert", None, "dp"),
            P("expert", None, "dp"),
            P("expert", "dp", None),
        ),
        out_specs=(P(("dp", "expert"), None), P(("dp", "expert"), None), P(("dp", "expert"), None)),
        check_vma=False,
    )
```
